32 devices in a mesh: seq: 4 (over y, x), ch: 8 (over z, core).
Axes of the slice: x: 2, y: 2, z: 4, core: 2. Of those that a mesh axis runs over, the one named last changes fastest.
Arguments:
- query: bfloat16 [512, 8192], P('seq', 'ch'), may hold values from -6 to 6
- key_in: bfloat16 [512, 8192], P('seq', 'ch'), may hold values from -6 to 6
- value: bfloat16 [512, 8192], P('seq', 'ch'), may hold values from -6 to 6
- out_grad: bfloat16 [512, 8192], P('seq', 'ch'), may hold values from -6 to 6
- filters: float32 [8192, 512], P(('ch', 'seq')), may hold values from -6 to 6
Outputs:
- grad_query: bfloat16 [512, 8192], P('seq', 'ch')
- grad_key: bfloat16 [512, 8192], P('seq', 'ch')
- grad_value: bfloat16 [512, 8192], P('seq', 'ch')
- filter_grad: float32 [8192, 512], P(('ch', 'seq'))
The draws below stay inside these ranges and needn't reach their ends.
All inputs are finite; a program needn't handle non-finite values.
Results may differ from the reference program's by a relative error of at most 0.0057.
Values may be sent and summed in bfloat16 or wider, within the bound.
A program may use at most 64 MiB of HBM per device.

```python
import math
import jax
import jax.numpy as jnp
from jax import lax

D = 8192
L = 512


def shard_levels(own_key, dims, pieces, low, top_value):
    gain = 1.0
    for position, parts in pieces:
        steps = jax.random.uniform(jax.random.fold_in(jax.random.fold_in(own_key, 6), position), (parts,), jnp.float32, low / len(pieces), top_value / len(pieces))
        gain = gain * jnp.repeat(jnp.exp(steps), dims[position] // parts).reshape((-1,) + (1,) * (len(dims) - 1 - position))
    return gain


def scatter_about(rng, shape, width, most, split=(), dtype=jnp.bfloat16):
    values = jax.random.normal(rng, shape, jnp.float32) * width
    if len(split) > 0:
        values = shard_levels(rng, shape, split, -0.22, 0.18) * values
    return jnp.clip(values, min=-most, max=most).astype(dtype)


def setup_inputs(seed: int = 0) -> dict:
    seeds = jax.random.split(jax.random.key(seed), 6)
    return {
        "query": scatter_about(seeds[0], (L, D), 1.0, 6.0, ((0, 4), (1, 8))),
        "key_in": scatter_about(seeds[1], (L, D), 1.0, 6.0, ((0, 4), (1, 8))),
        "value": scatter_about(seeds[2], (L, D), 1.0, 6.0, ((0, 4), (1, 8))),
        "out_grad": scatter_about(seeds[3], (L, D), 1.0, 6.0, ((0, 4), (1, 8))),
        "filters": scatter_about(seeds[4], (D, L), 1.0, 6.0, ((0, 32),), jnp.float32),
    }


def spectra_block(blocks):
    mixed_blk, gated_blk, filter_blk = blocks
    length = mixed_blk.shape[-1]
    padded_len = 2 * length
    factor = 1.0 / math.sqrt(length)
    spec_mixed = jnp.fft.rfft(mixed_blk.astype(jnp.float32), n=padded_len, axis=-1)
    spec_gated = jnp.fft.rfft(gated_blk.astype(jnp.float32), n=padded_len, axis=-1)
    spec_filter = jnp.fft.rfft(filter_blk.astype(jnp.float32), n=padded_len, axis=-1)
    conv_out = jnp.fft.irfft(spec_mixed * spec_filter, n=padded_len, axis=-1)[..., :length] * factor
    input_grad = jnp.fft.irfft(spec_gated * jnp.conj(spec_filter), n=padded_len, axis=-1)[..., :length] * factor
    filter_grad = jnp.fft.irfft(spec_gated * jnp.conj(spec_mixed), n=padded_len, axis=-1)[..., :length] * factor
    return (conv_out.astype(jnp.bfloat16), input_grad.astype(jnp.bfloat16), filter_grad.astype(jnp.float32))

def reference(query, key_in, value, out_grad, filters):
    seq_len, channels = query.shape
    block_size = min(256, channels)
    mixed = (key_in.astype(jnp.float32) * value.astype(jnp.float32)).astype(jnp.bfloat16)
    gated = (out_grad.astype(jnp.float32) * query.astype(jnp.float32)).astype(jnp.bfloat16)

    def blocked(array):
        return array.T.reshape(channels // block_size, block_size, seq_len)
    conv_out, input_grad, filter_grad = lax.map(spectra_block, (blocked(mixed), blocked(gated), filters.reshape(channels // block_size, block_size, seq_len)))
    conv_out = conv_out.reshape(channels, seq_len).T
    input_grad = input_grad.reshape(channels, seq_len).T
    grad_query = (out_grad.astype(jnp.float32) * conv_out.astype(jnp.float32)).astype(jnp.bfloat16)
    grad_key = (input_grad.astype(jnp.float32) * value.astype(jnp.float32)).astype(jnp.bfloat16)
    grad_value = (input_grad.astype(jnp.float32) * key_in.astype(jnp.float32)).astype(jnp.bfloat16)
    return (grad_query, grad_key, grad_value, filter_grad.reshape(channels, seq_len))
```

```python
import functools
import math

import jax
import jax.numpy as jnp
import ml_dtypes
import numpy as np
from jax import lax
from jax.experimental import pallas as pl
from jax.experimental.pallas import tpu as pltpu
from jax.sharding import PartitionSpec as P

HALVES = 2
MESH = pl.DeviceIdType.MESH


def split_bf16(table):
    high = table.astype(ml_dtypes.bfloat16)
    low = (table - high.astype(np.float64)).astype(ml_dtypes.bfloat16)
    return np.concatenate([high, low], axis=1)


def dft_tables(length):
    freq = 2 * np.arange(length)[:, None] + 1
    time = np.arange(length)[None, :]
    angle = np.pi * ((freq * time) % (4 * length)) / (2 * length)
    forward = np.concatenate([np.cos(angle), np.sin(angle)], axis=0)
    return split_bf16(forward), split_bf16(np.ascontiguousarray(forward.T))


def split_value(values):
    high = values.astype(jnp.bfloat16)
    low = (values - high.astype(jnp.float32)).astype(jnp.bfloat16)
    return high, low


def matmul(a, b):
    return jnp.dot(a, b, preferred_element_type=jnp.float32)


def matmul_t(a, b):
    return lax.dot_general(a, b, (((1,), (1,)), ((), ())), preferred_element_type=jnp.float32)


def partner(me, distance, n):
    total, bit = 0, 1
    while bit < n:
        digit = lax.rem(me // bit, 2)
        total = total + bit * (1 - digit if distance & bit else digit)
        bit *= 2
    return total


def fused_kernel(
    n,
    key_hbm, value_hbm, ograd_hbm, query_hbm, filt_hbm, fwd_hbm, inv_hbm,
    gq_hbm, gk_hbm, gv_hbm, fg_hbm,
    key, value, ograd, query, filt, fwd, inv,
    send, arrived, filt_spec, spec, prod, cross, result, back,
    gq, gk, gv, fg,
    load_sem, store_sem, send_sem, recv_sem,
):
    rows, channels = key.shape
    per_group, length = filt.shape
    width = per_group // HALVES
    scale = 1.0 / (length * math.sqrt(length))
    me = lax.axis_index("seq")
    others = list(range(n - 1, 0, -1))

    loads = [
        pltpu.make_async_copy(src, dst, load_sem.at[i])
        for i, (src, dst) in enumerate(
            [
                (key_hbm, key),
                (value_hbm, value),
                (ograd_hbm, ograd),
                (query_hbm, query),
                (filt_hbm, filt),
                (fwd_hbm, fwd),
                (inv_hbm, inv),
            ]
        )
    ]
    for load in loads:
        load.start()
    barrier = pltpu.get_barrier_semaphore()
    for d in others:
        pl.semaphore_signal(
            barrier, inc=1, device_id={"seq": partner(me, d, n)}, device_id_type=MESH
        )
    for load in loads[:4]:
        load.wait()

    def columns(owner, half):
        return pl.ds(pl.multiple_of(owner * per_group + half * width, width), width)

    def row_block(owner):
        return pl.ds(pl.multiple_of(owner * rows, rows), rows)

    def gates(half, owner):
        cols = columns(owner, half)
        mixed = key[:, cols].astype(jnp.float32) * value[:, cols].astype(jnp.float32)
        gated = ograd[:, cols].astype(jnp.float32) * query[:, cols].astype(jnp.float32)
        return mixed.astype(jnp.bfloat16), gated.astype(jnp.bfloat16)

    def fill(half, d):
        mixed, gated = gates(half, partner(me, d, n))
        send[half, d, :, :width] = mixed
        send[half, d, :, width:] = gated

    def out_copy(half, d):
        return pltpu.make_async_remote_copy(
            src_ref=send.at[half, d],
            dst_ref=arrived.at[half, row_block(me)],
            send_sem=send_sem.at[0, half, d],
            recv_sem=recv_sem.at[0, half, d],
            device_id={"seq": partner(me, d, n)},
            device_id_type=MESH,
        )

    def back_copy(half, d):
        return pltpu.make_async_remote_copy(
            src_ref=result.at[half, row_block(partner(me, d, n))],
            dst_ref=back.at[half, d],
            send_sem=send_sem.at[1, half, d],
            recv_sem=recv_sem.at[1, half, d],
            device_id={"seq": partner(me, d, n)},
            device_id_type=MESH,
        )

    for d in others:
        fill(0, d)
    pl.semaphore_wait(barrier, n - 1)
    sent = {}
    for half in range(HALVES):
        for d in others:
            if half > 0:
                fill(half, d)
            sent[0, half, d] = out_copy(half, d)
            sent[0, half, d].start()
    for half in range(HALVES):
        mixed, gated = gates(half, me)
        arrived[half, row_block(me), :width] = mixed
        arrived[half, row_block(me), width:] = gated

    loads[4].wait()
    loads[5].wait()
    f_high, f_low = split_value(filt[...])
    filt_spec[...] = (
        matmul_t(fwd[...], jnp.concatenate([f_high, f_high], axis=1))
        + matmul_t(fwd[:, :length], f_low)
    )
    loads[6].wait()

    chunk = min(64, length)
    for half in range(HALVES):
        for d in others:
            sent[0, half, d].wait_recv()
        data = arrived[half]
        spec[...] = matmul(fwd[...], jnp.concatenate([data, data], axis=0))
        fcols = slice(half * width, (half + 1) * width)
        double = 2 * length
        for start in range(0, length, chunk):
            cos_rows = slice(start, start + chunk)
            sin_rows = slice(length + start, length + start + chunk)
            cm, sm = spec[cos_rows, :width], spec[sin_rows, :width]
            cg, sg = spec[cos_rows, width:], spec[sin_rows, width:]
            ch, sh = filt_spec[cos_rows, fcols], filt_spec[sin_rows, fcols]
            parts = [
                (prod, cos_rows, slice(0, width), cm * ch - sm * sh),
                (prod, sin_rows, slice(0, width), cm * sh + sm * ch),
                (prod, cos_rows, slice(width, 2 * width), cg * ch + sg * sh),
                (prod, sin_rows, slice(width, 2 * width), sg * ch - cg * sh),
                (cross, cos_rows, fcols, cg * cm + sg * sm),
                (cross, sin_rows, fcols, sg * cm - cg * sm),
            ]
            for ref, to_rows, to_cols, values in parts:
                high, low = split_value(values)
                ref[0, to_rows, to_cols] = high
                ref[1, to_rows, to_cols] = low
        high, low = prod[0], prod[1]
        out = matmul(inv[...], jnp.concatenate([high, high], axis=0)) + matmul(
            inv[:, :double], low
        )
        result[half] = (out * scale).astype(jnp.bfloat16)
        for d in others:
            sent[1, half, d] = back_copy(half, d)
            sent[1, half, d].start()

    high, low = cross[0], cross[1]
    out = matmul(inv[...], jnp.concatenate([high, high], axis=0)) + matmul(inv[:, :double], low)
    fg[...] = (out * scale).T
    store_fg = pltpu.make_async_copy(fg, fg_hbm, store_sem.at[3])
    store_fg.start()

    def finish(half, owner, conv, igrad):
        cols = columns(owner, half)
        conv, igrad = conv.astype(jnp.float32), igrad.astype(jnp.float32)
        gq[:, cols] = (ograd[:, cols].astype(jnp.float32) * conv).astype(jnp.bfloat16)
        gk[:, cols] = (value[:, cols].astype(jnp.float32) * igrad).astype(jnp.bfloat16)
        gv[:, cols] = (key[:, cols].astype(jnp.float32) * igrad).astype(jnp.bfloat16)

    for half in range(HALVES):
        own = row_block(me)
        finish(half, me, result[half, own, :width], result[half, own, width:])
    for half in range(HALVES):
        for d in reversed(others):
            sent[1, half, d].wait_recv()
            finish(half, partner(me, d, n), back[half, d, :, :width], back[half, d, :, width:])
    stores = [
        pltpu.make_async_copy(src, dst, store_sem.at[i])
        for i, (src, dst) in enumerate([(gq, gq_hbm), (gk, gk_hbm), (gv, gv_hbm)])
    ]
    for store in stores:
        store.start()
    for copy in sent.values():
        copy.wait_send()
    for store in stores + [store_fg]:
        store.wait()


def fused(query, key_in, value, out_grad, filters):
    n = lax.axis_size("seq")
    rows, channels = query.shape
    per_group, length = filters.shape
    width = per_group // HALVES
    forward, inverse = dft_tables(length)
    bf16, f32 = jnp.bfloat16, jnp.float32
    gate = pltpu.VMEM((rows, channels), bf16)
    any_space = pl.BlockSpec(memory_space=pl.ANY)
    return pl.pallas_call(
        functools.partial(fused_kernel, n),
        out_shape=(
            jax.ShapeDtypeStruct((rows, channels), bf16),
            jax.ShapeDtypeStruct((rows, channels), bf16),
            jax.ShapeDtypeStruct((rows, channels), bf16),
            jax.ShapeDtypeStruct((per_group, length), f32),
        ),
        in_specs=[any_space] * 7,
        out_specs=(any_space,) * 4,
        scratch_shapes=[
            gate, gate, gate, gate,
            pltpu.VMEM((per_group, length), f32),
            pltpu.VMEM(forward.shape, bf16),
            pltpu.VMEM(inverse.shape, bf16),
            pltpu.VMEM((HALVES, n, rows, 2 * width), bf16),
            pltpu.VMEM((HALVES, length, 2 * width), bf16),
            pltpu.VMEM((2 * length, per_group), f32),
            pltpu.VMEM((2 * length, 2 * width), f32),
            pltpu.VMEM((2, 2 * length, 2 * width), bf16),
            pltpu.VMEM((2, 2 * length, per_group), bf16),
            pltpu.VMEM((HALVES, length, 2 * width), bf16),
            pltpu.VMEM((HALVES, n, rows, 2 * width), bf16),
            gate, gate, gate,
            pltpu.VMEM((per_group, length), f32),
            pltpu.SemaphoreType.DMA((7,)),
            pltpu.SemaphoreType.DMA((4,)),
            pltpu.SemaphoreType.DMA((2, HALVES, n)),
            pltpu.SemaphoreType.DMA((2, HALVES, n)),
        ],
        compiler_params=pltpu.CompilerParams(
            collective_id=0, has_side_effects=True, vmem_limit_bytes=48 * 1024 * 1024
        ),
        cost_estimate=pl.CostEstimate(
            flops=2 * 16 * 2 * length * length * per_group,
            bytes_accessed=12 * 1024 * 1024,
            transcendentals=0,
        ),
        name="hyena_bwd",
    )(key_in, value, out_grad, query, filters, jnp.asarray(forward), jnp.asarray(inverse))


def twiddle_tables(rows, cols, modulus, direction):
    row_index = lax.broadcasted_iota(jnp.int32, (rows, cols), 0)
    col_index = lax.broadcasted_iota(jnp.int32, (rows, cols), 1)
    angles = (
        direction * 2.0 * math.pi * (row_index * col_index % modulus).astype(jnp.float32) / modulus
    )
    return (jnp.cos(angles), jnp.sin(angles))


def complex_apply(real_part, imag_part, cosine, sines, form):
    highest = lax.Precision.HIGHEST
    out_real = jnp.einsum(form, real_part, cosine, precision=highest) - jnp.einsum(
        form, imag_part, sines, precision=highest
    )
    out_imag = jnp.einsum(form, real_part, sines, precision=highest) + jnp.einsum(
        form, imag_part, cosine, precision=highest
    )
    return (out_real, out_imag)


def transform(real_part, imag_part, direction):
    length = real_part.shape[-1]
    radix_one = math.gcd(length, 128)
    if length <= 256 or radix_one == 1:
        cosine, sines = twiddle_tables(length, length, length, direction)
        return complex_apply(real_part, imag_part, cosine, sines, "...j,kj->...k")
    radix_two = length // radix_one
    leading = real_part.shape[:-1]
    real_part = real_part.reshape(leading + (radix_one, radix_two))
    imag_part = imag_part.reshape(leading + (radix_one, radix_two))
    cosine, sines = twiddle_tables(radix_one, radix_one, radix_one, direction)
    real_part, imag_part = complex_apply(real_part, imag_part, cosine, sines, "...jm,kj->...km")
    cosine, sines = twiddle_tables(radix_one, radix_two, length, direction)
    real_part, imag_part = (
        real_part * cosine - imag_part * sines,
        real_part * sines + imag_part * cosine,
    )
    real_part, imag_part = transform(real_part, imag_part, direction)
    real_part = jnp.swapaxes(real_part, -1, -2).reshape(leading + (length,))
    imag_part = jnp.swapaxes(imag_part, -1, -2).reshape(leading + (length,))
    return (real_part, imag_part)


def mirrored(values):
    return jnp.roll(jnp.flip(values, -1), 1, -1)


def filter_work(mixed_part, gated_part, own_filter):
    length = mixed_part.shape[-1]
    padded_len = 2 * length
    factor = 1.0 / math.sqrt(length)

    def padded(values):
        widths = [(0, 0)] * (values.ndim - 1) + [(0, length)]
        return jnp.pad(values.astype(jnp.float32), widths)

    def inverse(real_part, imag_part):
        out_real, out_imag = transform(real_part, imag_part, 1.0)
        scale = factor / padded_len
        return (out_real[..., :length] * scale, out_imag[..., :length] * scale)

    both_re, both_im = transform(padded(mixed_part), padded(gated_part), -1.0)
    mirror_re, mirror_im = (mirrored(both_re), mirrored(both_im))
    mix_re = 0.5 * (both_re + mirror_re)
    mix_im = 0.5 * (both_im - mirror_im)
    gate_re = 0.5 * (both_im + mirror_im)
    gate_im = -0.5 * (both_re - mirror_re)
    filt_pad = padded(own_filter)
    filt_re, filt_im = transform(filt_pad, jnp.zeros_like(filt_pad), -1.0)
    conv_re = mix_re * filt_re - mix_im * filt_im
    conv_im = mix_re * filt_im + mix_im * filt_re
    back_re = gate_re * filt_re + gate_im * filt_im
    back_im = gate_im * filt_re - gate_re * filt_im
    conv_out, input_grad = inverse(conv_re - back_im, conv_im + back_re)
    filter_grad, unused = inverse(
        gate_re * mix_re + gate_im * mix_im, gate_im * mix_re - gate_re * mix_im
    )
    return (conv_out.astype(jnp.bfloat16), input_grad.astype(jnp.bfloat16), filter_grad)


def on_device(query, key_in, value, out_grad, filters):
    tok_rows, channels = query.shape
    groups = lax.axis_size("seq")
    per_group = channels // groups
    if groups & (groups - 1) == 0 and filters.shape[1] <= 1024 and per_group % 256 == 0:
        return fused(query, key_in, value, out_grad, filters)
    mixed = (key_in.astype(jnp.float32) * value.astype(jnp.float32)).astype(jnp.bfloat16)
    gated = (out_grad.astype(jnp.float32) * query.astype(jnp.float32)).astype(jnp.bfloat16)
    send_mixed = mixed.T.reshape(groups, per_group, tok_rows)
    send_gated = gated.T.reshape(groups, per_group, tok_rows)
    own_filter = filters[None]
    arrived_mix, arrived_gate = (
        lax.all_to_all(send_mixed, "seq", split_axis=0, concat_axis=2, tiled=True),
        lax.all_to_all(send_gated, "seq", split_axis=0, concat_axis=2, tiled=True),
    )
    conv_out, input_grad, filter_grad = filter_work(arrived_mix, arrived_gate, own_filter)
    back_conv, back_grad = (
        lax.all_to_all(conv_out, "seq", split_axis=2, concat_axis=0, tiled=True),
        lax.all_to_all(input_grad, "seq", split_axis=2, concat_axis=0, tiled=True),
    )
    back_conv = back_conv.reshape(channels, tok_rows).T
    back_grad = back_grad.reshape(channels, tok_rows).T
    grad_query = (out_grad.astype(jnp.float32) * back_conv.astype(jnp.float32)).astype(jnp.bfloat16)
    grad_key = (back_grad.astype(jnp.float32) * value.astype(jnp.float32)).astype(jnp.bfloat16)
    grad_value = (back_grad.astype(jnp.float32) * key_in.astype(jnp.float32)).astype(jnp.bfloat16)
    return (grad_query, grad_key, grad_value, filter_grad[0])


def solution(mesh):
    placed = (
        P("seq", "ch"),
        P("seq", "ch"),
        P("seq", "ch"),
        P("seq", "ch"),
        P(("ch", "seq"), None),
    )
    return jax.shard_map(
        on_device,
        mesh=mesh,
        in_specs=placed,
        out_specs=(P("seq", "ch"), P("seq", "ch"), P("seq", "ch"), P(("ch", "seq"), None)),
        check_vma=False,
    )
```

```python
import functools
import math

import jax
import jax.numpy as jnp
import ml_dtypes
import numpy as np
from jax import lax
from jax.experimental import pallas as pl
from jax.experimental.pallas import tpu as pltpu
from jax.sharding import PartitionSpec as P

HALVES = 2
GATE_STEPS = 2
VMEM_BYTES = 63 * 1024 * 1024
MESH = pl.DeviceIdType.MESH


def split_bf16(table):
    high = table.astype(ml_dtypes.bfloat16)
    low = (table - high.astype(np.float64)).astype(ml_dtypes.bfloat16)
    return np.concatenate([high, low], axis=1)


def dft_tables(length):
    freq = 2 * np.arange(length)[:, None] + 1
    time = np.arange(length)[None, :]
    angle = np.pi * ((freq * time) % (4 * length)) / (2 * length)
    forward = np.concatenate([np.cos(angle), np.sin(angle)], axis=0)
    return split_bf16(forward), split_bf16(np.ascontiguousarray(forward.T))


def split_value(values):
    high = values.astype(jnp.bfloat16)
    low = (values - high.astype(jnp.float32)).astype(jnp.bfloat16)
    return high, low


def matmul(a, b):
    return jnp.dot(a, b, preferred_element_type=jnp.float32)


def matmul_t(a, b):
    return lax.dot_general(a, b, (((1,), (1,)), ((), ())), preferred_element_type=jnp.float32)


def partner(me, distance, n):
    total, bit = 0, 1
    while bit < n:
        digit = lax.rem(me // bit, 2)
        total = total + bit * (1 - digit if distance & bit else digit)
        bit *= 2
    return total


def fused_kernel(
    n,
    key_hbm, value_hbm, ograd_hbm, query_hbm, filt_hbm, fwd_hbm, inv_hbm,
    back, fg_hbm,
    key, value, ograd, query, filt, fwd, inv,
    send, arrived, filt_spec, spec, prod, cross, result, fg,
    load_sem, store_sem, send_sem, recv_sem,
):
    rows, channels = key.shape
    per_group, length = filt.shape
    width = per_group // HALVES
    scale = 1.0 / (length * math.sqrt(length))
    me = lax.axis_index("seq")
    others = list(range(n - 1, 0, -1))

    loads = [
        pltpu.make_async_copy(src, dst, load_sem.at[i])
        for i, (src, dst) in enumerate(
            [
                (key_hbm, key),
                (value_hbm, value),
                (ograd_hbm, ograd),
                (query_hbm, query),
                (filt_hbm, filt),
                (fwd_hbm, fwd),
                (inv_hbm, inv),
            ]
        )
    ]
    for load in loads[:4]:
        load.start()
    barrier = pltpu.get_barrier_semaphore()
    for d in others:
        pl.semaphore_signal(
            barrier, inc=1, device_id={"seq": partner(me, d, n)}, device_id_type=MESH
        )
    for load in loads[:4]:
        load.wait()
    for load in loads[4:]:
        load.start()

    def columns(owner, half):
        return pl.ds(pl.multiple_of(owner * per_group + half * width, width), width)

    def row_block(owner):
        return pl.ds(pl.multiple_of(owner * rows, rows), rows)

    def gates(half, owner):
        cols = columns(owner, half)
        mixed = key[:, cols].astype(jnp.float32) * value[:, cols].astype(jnp.float32)
        gated = ograd[:, cols].astype(jnp.float32) * query[:, cols].astype(jnp.float32)
        return mixed.astype(jnp.bfloat16), gated.astype(jnp.bfloat16)

    def fill(half, d):
        mixed, gated = gates(half, partner(me, d, n))
        send[half, d, :, :width] = mixed
        send[half, d, :, width:] = gated

    def out_copy(half, d):
        return pltpu.make_async_remote_copy(
            src_ref=send.at[half, d],
            dst_ref=arrived.at[half, row_block(me)],
            send_sem=send_sem.at[0, half, d],
            recv_sem=recv_sem.at[0, half, d],
            device_id={"seq": partner(me, d, n)},
            device_id_type=MESH,
        )

    def back_copy(half, d):
        return pltpu.make_async_remote_copy(
            src_ref=result.at[half, row_block(partner(me, d, n))],
            dst_ref=back.at[half, me],
            send_sem=send_sem.at[1, half, d],
            recv_sem=recv_sem.at[1, half, d],
            device_id={"seq": partner(me, d, n)},
            device_id_type=MESH,
        )

    for d in others:
        fill(0, d)
    pl.semaphore_wait(barrier, n - 1)
    sent = {}
    for half in range(HALVES):
        for d in others:
            if half > 0:
                fill(half, d)
            sent[0, half, d] = out_copy(half, d)
            sent[0, half, d].start()
    for half in range(HALVES):
        mixed, gated = gates(half, me)
        arrived[half, row_block(me), :width] = mixed
        arrived[half, row_block(me), width:] = gated

    loads[4].wait()
    loads[5].wait()
    f_high, f_low = split_value(filt[...])
    filt_spec[...] = (
        matmul_t(fwd[...], jnp.concatenate([f_high, f_high], axis=1))
        + matmul_t(fwd[:, :length], f_low)
    )
    loads[6].wait()

    chunk = min(64, length)
    own = []
    for half in range(HALVES):
        for d in others:
            sent[0, half, d].wait_recv()
        data = arrived[half]
        spec[...] = matmul(fwd[...], jnp.concatenate([data, data], axis=0))
        fcols = slice(half * width, (half + 1) * width)
        double = 2 * length
        for start in range(0, length, chunk):
            cos_rows = slice(start, start + chunk)
            sin_rows = slice(length + start, length + start + chunk)
            cm, sm = spec[cos_rows, :width], spec[sin_rows, :width]
            cg, sg = spec[cos_rows, width:], spec[sin_rows, width:]
            ch, sh = filt_spec[cos_rows, fcols], filt_spec[sin_rows, fcols]
            parts = [
                (prod, cos_rows, slice(0, width), cm * ch - sm * sh),
                (prod, sin_rows, slice(0, width), cm * sh + sm * ch),
                (prod, cos_rows, slice(width, 2 * width), cg * ch + sg * sh),
                (prod, sin_rows, slice(width, 2 * width), sg * ch - cg * sh),
                (cross, cos_rows, fcols, cg * cm + sg * sm),
                (cross, sin_rows, fcols, sg * cm - cg * sm),
            ]
            for ref, to_rows, to_cols, values in parts:
                high, low = split_value(values)
                ref[0, to_rows, to_cols] = high
                ref[1, to_rows, to_cols] = low
        high, low = prod[0], prod[1]
        out = matmul(inv[...], jnp.concatenate([high, high], axis=0)) + matmul(
            inv[:, :double], low
        )
        result[half] = (out * scale).astype(jnp.bfloat16)
        for d in others:
            sent[1, half, d] = back_copy(half, d)
            sent[1, half, d].start()
        own.append(
            pltpu.make_async_copy(
                result.at[half, row_block(me)], back.at[half, me], store_sem.at[1 + half]
            )
        )
        own[-1].start()

    high, low = cross[0], cross[1]
    out = matmul(inv[...], jnp.concatenate([high, high], axis=0)) + matmul(inv[:, :double], low)
    fg[...] = (out * scale).T
    store_fg = pltpu.make_async_copy(fg, fg_hbm, store_sem.at[0])
    store_fg.start()

    for half in range(HALVES):
        for d in others:
            sent[1, half, d].wait_recv()
    for copy in sent.values():
        copy.wait_send()
    for store in own + [store_fg]:
        store.wait()


def gate_kernel(
    key_hbm, value_hbm, ograd_hbm, back_hbm, fg_in, gq_hbm, gk_hbm, gv_hbm, fg_out,
    key, value, ograd, back, gq, gk, gv, load_sem, store_sem,
):
    pieces, n, rows, double = back.shape
    width = double // 2
    store_fg = pltpu.make_async_copy(fg_in, fg_out, store_sem.at[0, 0])
    block = rows // GATE_STEPS
    loads = []
    for step in range(GATE_STEPS):
        part = pl.ds(step * block, block)
        pairs = [
            (back_hbm.at[:, :, part], back.at[:, :, part]),
            (key_hbm.at[part], key.at[part]),
            (value_hbm.at[part], value.at[part]),
            (ograd_hbm.at[part], ograd.at[part]),
        ]
        loads.append(
            [pltpu.make_async_copy(s, d, load_sem.at[step, i]) for i, (s, d) in enumerate(pairs)]
        )
        for load in loads[-1]:
            load.start()
    store_fg.start()
    stores = [store_fg]
    for step in range(GATE_STEPS):
        part = pl.ds(step * block, block)
        for load in loads[step]:
            load.wait()
        for owner in range(n):
            for half in range(pieces):
                first = (owner * pieces + half) * width
                cols = slice(first, first + width)
                conv = back[half, owner, part, :width].astype(jnp.float32)
                igrad = back[half, owner, part, width:].astype(jnp.float32)
                gq[part, cols] = (ograd[part, cols].astype(jnp.float32) * conv).astype(gq.dtype)
                gk[part, cols] = (value[part, cols].astype(jnp.float32) * igrad).astype(gk.dtype)
                gv[part, cols] = (key[part, cols].astype(jnp.float32) * igrad).astype(gv.dtype)
        for i, (src, dst) in enumerate([(gq, gq_hbm), (gk, gk_hbm), (gv, gv_hbm)]):
            store = pltpu.make_async_copy(src.at[part], dst.at[part], store_sem.at[step, 1 + i])
            store.start()
            stores.append(store)
    for store in stores:
        store.wait()


def fused(query, key_in, value, out_grad, filters):
    n = lax.axis_size("seq")
    rows, channels = query.shape
    per_group, length = filters.shape
    width = per_group // HALVES
    forward, inverse = dft_tables(length)
    bf16, f32 = jnp.bfloat16, jnp.float32
    gate = pltpu.VMEM((rows, channels), bf16)
    gate_shape = jax.ShapeDtypeStruct((rows, channels), bf16)
    back_shape = (HALVES, n, rows, 2 * width)
    fg_shape = jax.ShapeDtypeStruct((per_group, length), f32)
    any_space = pl.BlockSpec(memory_space=pl.ANY)
    hbm = pl.BlockSpec(memory_space=pltpu.HBM)
    back, filter_grad = pl.pallas_call(
        functools.partial(fused_kernel, n),
        out_shape=(jax.ShapeDtypeStruct(back_shape, bf16), fg_shape),
        in_specs=[hbm] * 7,
        out_specs=(any_space,) * 2,
        scratch_shapes=[
            gate, gate, gate, gate,
            pltpu.VMEM((per_group, length), f32),
            pltpu.VMEM(forward.shape, bf16),
            pltpu.VMEM(inverse.shape, bf16),
            pltpu.VMEM((HALVES, n, rows, 2 * width), bf16),
            pltpu.VMEM((HALVES, length, 2 * width), bf16),
            pltpu.VMEM((2 * length, per_group), f32),
            pltpu.VMEM((2 * length, 2 * width), f32),
            pltpu.VMEM((2, 2 * length, 2 * width), bf16),
            pltpu.VMEM((2, 2 * length, per_group), bf16),
            pltpu.VMEM((HALVES, length, 2 * width), bf16),
            pltpu.VMEM((per_group, length), f32),
            pltpu.SemaphoreType.DMA((7,)),
            pltpu.SemaphoreType.DMA((1 + HALVES,)),
            pltpu.SemaphoreType.DMA((2, HALVES, n)),
            pltpu.SemaphoreType.DMA((2, HALVES, n)),
        ],
        compiler_params=pltpu.CompilerParams(
            collective_id=0, has_side_effects=True, vmem_limit_bytes=VMEM_BYTES
        ),
        cost_estimate=pl.CostEstimate(
            flops=2 * 16 * 2 * length * length * per_group,
            bytes_accessed=12 * 1024 * 1024,
            transcendentals=0,
        ),
        name="hyena_bwd",
    )(key_in, value, out_grad, query, filters, jnp.asarray(forward), jnp.asarray(inverse))
    return pl.pallas_call(
        gate_kernel,
        out_shape=(gate_shape, gate_shape, gate_shape, fg_shape),
        in_specs=[hbm] * 3 + [any_space] * 2,
        out_specs=(hbm,) * 4,
        scratch_shapes=[
            gate, gate, gate,
            pltpu.VMEM(back_shape, bf16),
            gate, gate, gate,
            pltpu.SemaphoreType.DMA((GATE_STEPS, 4)),
            pltpu.SemaphoreType.DMA((GATE_STEPS, 4)),
        ],
        compiler_params=pltpu.CompilerParams(vmem_limit_bytes=VMEM_BYTES),
        cost_estimate=pl.CostEstimate(
            flops=6 * rows * channels, bytes_accessed=4 * 1024 * 1024, transcendentals=0
        ),
        name="output_gates",
    )(key_in, value, out_grad, back, filter_grad)


def twiddle_tables(rows, cols, modulus, direction):
    row_index = lax.broadcasted_iota(jnp.int32, (rows, cols), 0)
    col_index = lax.broadcasted_iota(jnp.int32, (rows, cols), 1)
    angles = (
        direction * 2.0 * math.pi * (row_index * col_index % modulus).astype(jnp.float32) / modulus
    )
    return (jnp.cos(angles), jnp.sin(angles))


def complex_apply(real_part, imag_part, cosine, sines, form):
    highest = lax.Precision.HIGHEST
    out_real = jnp.einsum(form, real_part, cosine, precision=highest) - jnp.einsum(
        form, imag_part, sines, precision=highest
    )
    out_imag = jnp.einsum(form, real_part, sines, precision=highest) + jnp.einsum(
        form, imag_part, cosine, precision=highest
    )
    return (out_real, out_imag)


def transform(real_part, imag_part, direction):
    length = real_part.shape[-1]
    radix_one = math.gcd(length, 128)
    if length <= 256 or radix_one == 1:
        cosine, sines = twiddle_tables(length, length, length, direction)
        return complex_apply(real_part, imag_part, cosine, sines, "...j,kj->...k")
    radix_two = length // radix_one
    leading = real_part.shape[:-1]
    real_part = real_part.reshape(leading + (radix_one, radix_two))
    imag_part = imag_part.reshape(leading + (radix_one, radix_two))
    cosine, sines = twiddle_tables(radix_one, radix_one, radix_one, direction)
    real_part, imag_part = complex_apply(real_part, imag_part, cosine, sines, "...jm,kj->...km")
    cosine, sines = twiddle_tables(radix_one, radix_two, length, direction)
    real_part, imag_part = (
        real_part * cosine - imag_part * sines,
        real_part * sines + imag_part * cosine,
    )
    real_part, imag_part = transform(real_part, imag_part, direction)
    real_part = jnp.swapaxes(real_part, -1, -2).reshape(leading + (length,))
    imag_part = jnp.swapaxes(imag_part, -1, -2).reshape(leading + (length,))
    return (real_part, imag_part)


def mirrored(values):
    return jnp.roll(jnp.flip(values, -1), 1, -1)


def filter_work(mixed_part, gated_part, own_filter):
    length = mixed_part.shape[-1]
    padded_len = 2 * length
    factor = 1.0 / math.sqrt(length)

    def padded(values):
        widths = [(0, 0)] * (values.ndim - 1) + [(0, length)]
        return jnp.pad(values.astype(jnp.float32), widths)

    def inverse(real_part, imag_part):
        out_real, out_imag = transform(real_part, imag_part, 1.0)
        scale = factor / padded_len
        return (out_real[..., :length] * scale, out_imag[..., :length] * scale)

    both_re, both_im = transform(padded(mixed_part), padded(gated_part), -1.0)
    mirror_re, mirror_im = (mirrored(both_re), mirrored(both_im))
    mix_re = 0.5 * (both_re + mirror_re)
    mix_im = 0.5 * (both_im - mirror_im)
    gate_re = 0.5 * (both_im + mirror_im)
    gate_im = -0.5 * (both_re - mirror_re)
    filt_pad = padded(own_filter)
    filt_re, filt_im = transform(filt_pad, jnp.zeros_like(filt_pad), -1.0)
    conv_re = mix_re * filt_re - mix_im * filt_im
    conv_im = mix_re * filt_im + mix_im * filt_re
    back_re = gate_re * filt_re + gate_im * filt_im
    back_im = gate_im * filt_re - gate_re * filt_im
    conv_out, input_grad = inverse(conv_re - back_im, conv_im + back_re)
    filter_grad, unused = inverse(
        gate_re * mix_re + gate_im * mix_im, gate_im * mix_re - gate_re * mix_im
    )
    return (conv_out.astype(jnp.bfloat16), input_grad.astype(jnp.bfloat16), filter_grad)


def on_device(query, key_in, value, out_grad, filters):
    tok_rows, channels = query.shape
    groups = lax.axis_size("seq")
    per_group = channels // groups
    if groups & (groups - 1) == 0 and filters.shape[1] <= 1024 and per_group % 256 == 0:
        return fused(query, key_in, value, out_grad, filters)
    mixed = (key_in.astype(jnp.float32) * value.astype(jnp.float32)).astype(jnp.bfloat16)
    gated = (out_grad.astype(jnp.float32) * query.astype(jnp.float32)).astype(jnp.bfloat16)
    send_mixed = mixed.T.reshape(groups, per_group, tok_rows)
    send_gated = gated.T.reshape(groups, per_group, tok_rows)
    own_filter = filters[None]
    arrived_mix, arrived_gate = (
        lax.all_to_all(send_mixed, "seq", split_axis=0, concat_axis=2, tiled=True),
        lax.all_to_all(send_gated, "seq", split_axis=0, concat_axis=2, tiled=True),
    )
    conv_out, input_grad, filter_grad = filter_work(arrived_mix, arrived_gate, own_filter)
    back_conv, back_grad = (
        lax.all_to_all(conv_out, "seq", split_axis=2, concat_axis=0, tiled=True),
        lax.all_to_all(input_grad, "seq", split_axis=2, concat_axis=0, tiled=True),
    )
    back_conv = back_conv.reshape(channels, tok_rows).T
    back_grad = back_grad.reshape(channels, tok_rows).T
    grad_query = (out_grad.astype(jnp.float32) * back_conv.astype(jnp.float32)).astype(jnp.bfloat16)
    grad_key = (back_grad.astype(jnp.float32) * value.astype(jnp.float32)).astype(jnp.bfloat16)
    grad_value = (back_grad.astype(jnp.float32) * key_in.astype(jnp.float32)).astype(jnp.bfloat16)
    return (grad_query, grad_key, grad_value, filter_grad[0])


def solution(mesh):
    placed = (
        P("seq", "ch"),
        P("seq", "ch"),
        P("seq", "ch"),
        P("seq", "ch"),
        P(("ch", "seq"), None),
    )
    return jax.shard_map(
        on_device,
        mesh=mesh,
        in_specs=placed,
        out_specs=(P("seq", "ch"), P("seq", "ch"), P("seq", "ch"), P(("ch", "seq"), None)),
        check_vma=False,
    )
```

```python
import functools
import math

import jax
import jax.numpy as jnp
import ml_dtypes
import numpy as np
from jax import lax
from jax.experimental import pallas as pl
from jax.experimental.pallas import tpu as pltpu
from jax.sharding import PartitionSpec as P

HALVES = 2
GATE_STEPS = 2
VMEM_BYTES = 63 * 1024 * 1024
MESH = pl.DeviceIdType.MESH


def split_bf16(table):
    high = table.astype(ml_dtypes.bfloat16)
    low = (table - high.astype(np.float64)).astype(ml_dtypes.bfloat16)
    return np.concatenate([high, low], axis=1)


def dft_tables(length):
    freq = 2 * np.arange(length)[:, None] + 1
    time = np.arange(length)[None, :]
    angle = np.pi * ((freq * time) % (4 * length)) / (2 * length)
    forward = np.concatenate([np.cos(angle), np.sin(angle)], axis=0)
    return split_bf16(forward), split_bf16(np.ascontiguousarray(forward.T))


def split_value(values):
    high = values.astype(jnp.bfloat16)
    low = (values - high.astype(jnp.float32)).astype(jnp.bfloat16)
    return high, low


def matmul(a, b):
    return jnp.dot(a, b, preferred_element_type=jnp.float32)


def matmul_t(a, b):
    return lax.dot_general(a, b, (((1,), (1,)), ((), ())), preferred_element_type=jnp.float32)


def partner(me, distance, n):
    total, bit = 0, 1
    while bit < n:
        digit = lax.rem(me // bit, 2)
        total = total + bit * (1 - digit if distance & bit else digit)
        bit *= 2
    return total


def fused_kernel(
    n,
    key_hbm, value_hbm, ograd_hbm, query_hbm, filt_hbm, fwd_hbm, inv_hbm,
    back, fg_hbm,
    key, value, ograd, query, filt, fwd, inv,
    send, arrived, filt_spec, spec, prod, cross, result, fg,
    load_sem, store_sem, send_sem, recv_sem,
):
    rows, channels = key.shape
    per_group, length = filt.shape
    width = per_group // HALVES
    scale = 1.0 / (length * math.sqrt(length))
    me = lax.axis_index("seq")
    others = list(range(n - 1, 0, -1))

    loads = [
        pltpu.make_async_copy(src, dst, load_sem.at[i])
        for i, (src, dst) in enumerate(
            [
                (key_hbm, key),
                (value_hbm, value),
                (ograd_hbm, ograd),
                (query_hbm, query),
                (filt_hbm, filt),
                (fwd_hbm, fwd),
                (inv_hbm, inv),
            ]
        )
    ]
    for load in loads[:4]:
        load.start()
    barrier = pltpu.get_barrier_semaphore()
    for d in others:
        pl.semaphore_signal(
            barrier, inc=1, device_id={"seq": partner(me, d, n)}, device_id_type=MESH
        )
    for load in loads[:4]:
        load.wait()
    for load in loads[4:]:
        load.start()

    def columns(owner, half):
        return pl.ds(pl.multiple_of(owner * per_group + half * width, width), width)

    def row_block(owner):
        return pl.ds(pl.multiple_of(owner * rows, rows), rows)

    def gates(half, owner):
        cols = columns(owner, half)
        mixed = key[:, cols].astype(jnp.float32) * value[:, cols].astype(jnp.float32)
        gated = ograd[:, cols].astype(jnp.float32) * query[:, cols].astype(jnp.float32)
        return mixed.astype(jnp.bfloat16), gated.astype(jnp.bfloat16)

    def fill(half, d):
        mixed, gated = gates(half, partner(me, d, n))
        send[half, d, :, :width] = mixed
        send[half, d, :, width:] = gated

    def out_copy(half, d):
        return pltpu.make_async_remote_copy(
            src_ref=send.at[half, d],
            dst_ref=arrived.at[half, row_block(me)],
            send_sem=send_sem.at[0, half, d],
            recv_sem=recv_sem.at[0, half, d],
            device_id={"seq": partner(me, d, n)},
            device_id_type=MESH,
        )

    def back_copy(half, d):
        return pltpu.make_async_remote_copy(
            src_ref=result.at[half, row_block(partner(me, d, n))],
            dst_ref=back.at[half, me],
            send_sem=send_sem.at[1, half, d],
            recv_sem=recv_sem.at[1, half, d],
            device_id={"seq": partner(me, d, n)},
            device_id_type=MESH,
        )

    for d in others:
        fill(0, d)
    pl.semaphore_wait(barrier, n - 1)
    sent = {}
    for half in range(HALVES):
        for d in others:
            if half > 0:
                fill(half, d)
            sent[0, half, d] = out_copy(half, d)
            sent[0, half, d].start()
    for half in range(HALVES):
        mixed, gated = gates(half, me)
        arrived[half, row_block(me), :width] = mixed
        arrived[half, row_block(me), width:] = gated

    loads[4].wait()
    loads[5].wait()
    f_high, f_low = split_value(filt[...])
    filt_spec[...] = (
        matmul_t(fwd[...], jnp.concatenate([f_high, f_high], axis=1))
        + matmul_t(fwd[:, :length], f_low)
    )
    loads[6].wait()

    chunk = min(64, length)
    own = []
    for half in range(HALVES):
        for d in others:
            sent[0, half, d].wait_recv()
        data = arrived[half]
        spec[...] = matmul(fwd[...], jnp.concatenate([data, data], axis=0))
        fcols = slice(half * width, (half + 1) * width)
        double = 2 * length
        for start in range(0, length, chunk):
            cos_rows = slice(start, start + chunk)
            sin_rows = slice(length + start, length + start + chunk)
            cm, sm = spec[cos_rows, :width], spec[sin_rows, :width]
            cg, sg = spec[cos_rows, width:], spec[sin_rows, width:]
            ch, sh = filt_spec[cos_rows, fcols], filt_spec[sin_rows, fcols]
            parts = [
                (prod, cos_rows, slice(0, width), cm * ch - sm * sh),
                (prod, sin_rows, slice(0, width), cm * sh + sm * ch),
                (prod, cos_rows, slice(width, 2 * width), cg * ch + sg * sh),
                (prod, sin_rows, slice(width, 2 * width), sg * ch - cg * sh),
                (cross, cos_rows, fcols, cg * cm + sg * sm),
                (cross, sin_rows, fcols, sg * cm - cg * sm),
            ]
            for ref, to_rows, to_cols, values in parts:
                high, low = split_value(values)
                ref[0, to_rows, to_cols] = high
                ref[1, to_rows, to_cols] = low
        high, low = prod[0], prod[1]
        out = matmul(inv[...], jnp.concatenate([high, high], axis=0)) + matmul(
            inv[:, :double], low
        )
        result[half] = (out * scale).astype(jnp.bfloat16)
        for d in others:
            sent[1, half, d] = back_copy(half, d)
            sent[1, half, d].start()
        own.append(
            pltpu.make_async_copy(
                result.at[half, row_block(me)], back.at[half, me], store_sem.at[1 + half]
            )
        )
        own[-1].start()

    high, low = cross[0], cross[1]
    out = matmul(inv[...], jnp.concatenate([high, high], axis=0)) + matmul(inv[:, :double], low)
    fg[...] = (out * scale).T
    store_fg = pltpu.make_async_copy(fg, fg_hbm, store_sem.at[0])
    store_fg.start()

    for half in range(HALVES):
        for d in others:
            sent[1, half, d].wait_recv()
    for copy in sent.values():
        copy.wait_send()
    for store in own + [store_fg]:
        store.wait()


def gate_kernel(
    key_hbm, value_hbm, ograd_hbm, back_hbm, fg_in, gq_hbm, gk_hbm, gv_hbm, fg_out,
    key, value, ograd, back, gq, gk, gv, fg, load_sem, store_sem,
):
    pieces, n, rows, double = back.shape
    width = double // 2
    load_fg = pltpu.make_async_copy(fg_in, fg, load_sem.at[0, 4])
    store_fg = pltpu.make_async_copy(fg, fg_out, store_sem.at[0, 0])
    block = rows // GATE_STEPS
    loads = []
    for step in range(GATE_STEPS):
        part = pl.ds(step * block, block)
        pairs = [
            (back_hbm.at[:, :, part], back.at[:, :, part]),
            (key_hbm.at[part], key.at[part]),
            (value_hbm.at[part], value.at[part]),
            (ograd_hbm.at[part], ograd.at[part]),
        ]
        loads.append(
            [pltpu.make_async_copy(s, d, load_sem.at[step, i]) for i, (s, d) in enumerate(pairs)]
        )
        for load in loads[-1]:
            load.start()
        if step == 0:
            load_fg.start()
    stores = [store_fg]
    for step in range(GATE_STEPS):
        part = pl.ds(step * block, block)
        for load in loads[step]:
            load.wait()
        for owner in range(n):
            for half in range(pieces):
                first = (owner * pieces + half) * width
                cols = slice(first, first + width)
                conv = back[half, owner, part, :width].astype(jnp.float32)
                igrad = back[half, owner, part, width:].astype(jnp.float32)
                gq[part, cols] = (ograd[part, cols].astype(jnp.float32) * conv).astype(gq.dtype)
                gk[part, cols] = (value[part, cols].astype(jnp.float32) * igrad).astype(gk.dtype)
                gv[part, cols] = (key[part, cols].astype(jnp.float32) * igrad).astype(gv.dtype)
        for i, (src, dst) in enumerate([(gq, gq_hbm), (gk, gk_hbm), (gv, gv_hbm)]):
            store = pltpu.make_async_copy(src.at[part], dst.at[part], store_sem.at[step, 1 + i])
            store.start()
            stores.append(store)
        if step == 0:
            load_fg.wait()
            store_fg.start()
    for store in stores:
        store.wait()


def fused(query, key_in, value, out_grad, filters):
    n = lax.axis_size("seq")
    rows, channels = query.shape
    per_group, length = filters.shape
    width = per_group // HALVES
    forward, inverse = dft_tables(length)
    bf16, f32 = jnp.bfloat16, jnp.float32
    gate = pltpu.VMEM((rows, channels), bf16)
    gate_shape = jax.ShapeDtypeStruct((rows, channels), bf16)
    back_shape = (HALVES, n, rows, 2 * width)
    fg_shape = jax.ShapeDtypeStruct((per_group, length), f32)
    any_space = pl.BlockSpec(memory_space=pl.ANY)
    hbm = pl.BlockSpec(memory_space=pltpu.HBM)
    back, filter_grad = pl.pallas_call(
        functools.partial(fused_kernel, n),
        out_shape=(jax.ShapeDtypeStruct(back_shape, bf16), fg_shape),
        in_specs=[hbm] * 7,
        out_specs=(any_space,) * 2,
        scratch_shapes=[
            gate, gate, gate, gate,
            pltpu.VMEM((per_group, length), f32),
            pltpu.VMEM(forward.shape, bf16),
            pltpu.VMEM(inverse.shape, bf16),
            pltpu.VMEM((HALVES, n, rows, 2 * width), bf16),
            pltpu.VMEM((HALVES, length, 2 * width), bf16),
            pltpu.VMEM((2 * length, per_group), f32),
            pltpu.VMEM((2 * length, 2 * width), f32),
            pltpu.VMEM((2, 2 * length, 2 * width), bf16),
            pltpu.VMEM((2, 2 * length, per_group), bf16),
            pltpu.VMEM((HALVES, length, 2 * width), bf16),
            pltpu.VMEM((per_group, length), f32),
            pltpu.SemaphoreType.DMA((7,)),
            pltpu.SemaphoreType.DMA((1 + HALVES,)),
            pltpu.SemaphoreType.DMA((2, HALVES, n)),
            pltpu.SemaphoreType.DMA((2, HALVES, n)),
        ],
        compiler_params=pltpu.CompilerParams(
            collective_id=0, has_side_effects=True, vmem_limit_bytes=VMEM_BYTES
        ),
        cost_estimate=pl.CostEstimate(
            flops=2 * 16 * 2 * length * length * per_group,
            bytes_accessed=12 * 1024 * 1024,
            transcendentals=0,
        ),
        name="hyena_bwd",
    )(key_in, value, out_grad, query, filters, jnp.asarray(forward), jnp.asarray(inverse))
    return pl.pallas_call(
        gate_kernel,
        out_shape=(gate_shape, gate_shape, gate_shape, fg_shape),
        in_specs=[hbm] * 3 + [any_space] * 2,
        out_specs=(hbm,) * 4,
        scratch_shapes=[
            gate, gate, gate,
            pltpu.VMEM(back_shape, bf16),
            gate, gate, gate,
            pltpu.VMEM((per_group, length), f32),
            pltpu.SemaphoreType.DMA((GATE_STEPS, 5)),
            pltpu.SemaphoreType.DMA((GATE_STEPS, 4)),
        ],
        compiler_params=pltpu.CompilerParams(vmem_limit_bytes=VMEM_BYTES),
        cost_estimate=pl.CostEstimate(
            flops=6 * rows * channels, bytes_accessed=4 * 1024 * 1024, transcendentals=0
        ),
        name="output_gates",
    )(key_in, value, out_grad, back, filter_grad)


def twiddle_tables(rows, cols, modulus, direction):
    row_index = lax.broadcasted_iota(jnp.int32, (rows, cols), 0)
    col_index = lax.broadcasted_iota(jnp.int32, (rows, cols), 1)
    angles = (
        direction * 2.0 * math.pi * (row_index * col_index % modulus).astype(jnp.float32) / modulus
    )
    return (jnp.cos(angles), jnp.sin(angles))


def complex_apply(real_part, imag_part, cosine, sines, form):
    highest = lax.Precision.HIGHEST
    out_real = jnp.einsum(form, real_part, cosine, precision=highest) - jnp.einsum(
        form, imag_part, sines, precision=highest
    )
    out_imag = jnp.einsum(form, real_part, sines, precision=highest) + jnp.einsum(
        form, imag_part, cosine, precision=highest
    )
    return (out_real, out_imag)


def transform(real_part, imag_part, direction):
    length = real_part.shape[-1]
    radix_one = math.gcd(length, 128)
    if length <= 256 or radix_one == 1:
        cosine, sines = twiddle_tables(length, length, length, direction)
        return complex_apply(real_part, imag_part, cosine, sines, "...j,kj->...k")
    radix_two = length // radix_one
    leading = real_part.shape[:-1]
    real_part = real_part.reshape(leading + (radix_one, radix_two))
    imag_part = imag_part.reshape(leading + (radix_one, radix_two))
    cosine, sines = twiddle_tables(radix_one, radix_one, radix_one, direction)
    real_part, imag_part = complex_apply(real_part, imag_part, cosine, sines, "...jm,kj->...km")
    cosine, sines = twiddle_tables(radix_one, radix_two, length, direction)
    real_part, imag_part = (
        real_part * cosine - imag_part * sines,
        real_part * sines + imag_part * cosine,
    )
    real_part, imag_part = transform(real_part, imag_part, direction)
    real_part = jnp.swapaxes(real_part, -1, -2).reshape(leading + (length,))
    imag_part = jnp.swapaxes(imag_part, -1, -2).reshape(leading + (length,))
    return (real_part, imag_part)


def mirrored(values):
    return jnp.roll(jnp.flip(values, -1), 1, -1)


def filter_work(mixed_part, gated_part, own_filter):
    length = mixed_part.shape[-1]
    padded_len = 2 * length
    factor = 1.0 / math.sqrt(length)

    def padded(values):
        widths = [(0, 0)] * (values.ndim - 1) + [(0, length)]
        return jnp.pad(values.astype(jnp.float32), widths)

    def inverse(real_part, imag_part):
        out_real, out_imag = transform(real_part, imag_part, 1.0)
        scale = factor / padded_len
        return (out_real[..., :length] * scale, out_imag[..., :length] * scale)

    both_re, both_im = transform(padded(mixed_part), padded(gated_part), -1.0)
    mirror_re, mirror_im = (mirrored(both_re), mirrored(both_im))
    mix_re = 0.5 * (both_re + mirror_re)
    mix_im = 0.5 * (both_im - mirror_im)
    gate_re = 0.5 * (both_im + mirror_im)
    gate_im = -0.5 * (both_re - mirror_re)
    filt_pad = padded(own_filter)
    filt_re, filt_im = transform(filt_pad, jnp.zeros_like(filt_pad), -1.0)
    conv_re = mix_re * filt_re - mix_im * filt_im
    conv_im = mix_re * filt_im + mix_im * filt_re
    back_re = gate_re * filt_re + gate_im * filt_im
    back_im = gate_im * filt_re - gate_re * filt_im
    conv_out, input_grad = inverse(conv_re - back_im, conv_im + back_re)
    filter_grad, unused = inverse(
        gate_re * mix_re + gate_im * mix_im, gate_im * mix_re - gate_re * mix_im
    )
    return (conv_out.astype(jnp.bfloat16), input_grad.astype(jnp.bfloat16), filter_grad)


def on_device(query, key_in, value, out_grad, filters):
    tok_rows, channels = query.shape
    groups = lax.axis_size("seq")
    per_group = channels // groups
    if groups & (groups - 1) == 0 and filters.shape[1] <= 1024 and per_group % 256 == 0:
        return fused(query, key_in, value, out_grad, filters)
    mixed = (key_in.astype(jnp.float32) * value.astype(jnp.float32)).astype(jnp.bfloat16)
    gated = (out_grad.astype(jnp.float32) * query.astype(jnp.float32)).astype(jnp.bfloat16)
    send_mixed = mixed.T.reshape(groups, per_group, tok_rows)
    send_gated = gated.T.reshape(groups, per_group, tok_rows)
    own_filter = filters[None]
    arrived_mix, arrived_gate = (
        lax.all_to_all(send_mixed, "seq", split_axis=0, concat_axis=2, tiled=True),
        lax.all_to_all(send_gated, "seq", split_axis=0, concat_axis=2, tiled=True),
    )
    conv_out, input_grad, filter_grad = filter_work(arrived_mix, arrived_gate, own_filter)
    back_conv, back_grad = (
        lax.all_to_all(conv_out, "seq", split_axis=2, concat_axis=0, tiled=True),
        lax.all_to_all(input_grad, "seq", split_axis=2, concat_axis=0, tiled=True),
    )
    back_conv = back_conv.reshape(channels, tok_rows).T
    back_grad = back_grad.reshape(channels, tok_rows).T
    grad_query = (out_grad.astype(jnp.float32) * back_conv.astype(jnp.float32)).astype(jnp.bfloat16)
    grad_key = (back_grad.astype(jnp.float32) * value.astype(jnp.float32)).astype(jnp.bfloat16)
    grad_value = (back_grad.astype(jnp.float32) * key_in.astype(jnp.float32)).astype(jnp.bfloat16)
    return (grad_query, grad_key, grad_value, filter_grad[0])


def solution(mesh):
    placed = (
        P("seq", "ch"),
        P("seq", "ch"),
        P("seq", "ch"),
        P("seq", "ch"),
        P(("ch", "seq"), None),
    )
    return jax.shard_map(
        on_device,
        mesh=mesh,
        in_specs=placed,
        out_specs=(P("seq", "ch"), P("seq", "ch"), P("seq", "ch"), P(("ch", "seq"), None)),
        check_vma=False,
    )
```

```python
import functools
import math

import jax
import jax.numpy as jnp
import ml_dtypes
import numpy as np
from jax import lax
from jax.experimental import pallas as pl
from jax.experimental.pallas import tpu as pltpu
from jax.sharding import PartitionSpec as P

HALVES = 2
GATE_STEPS = 2
VMEM_BYTES = 63 * 1024 * 1024
MESH = pl.DeviceIdType.MESH


def split_bf16(table):
    high = table.astype(ml_dtypes.bfloat16)
    low = (table - high.astype(np.float64)).astype(ml_dtypes.bfloat16)
    return np.concatenate([high, low], axis=1)


def dft_tables(length):
    freq = 2 * np.arange(length // 2)[:, None] + 1
    forward, inverse = [], []
    for parity in range(2):
        time = np.arange(parity, length, 2)[None, :]
        angle = np.pi * ((freq * time) % (4 * length)) / (2 * length)
        table = np.concatenate([np.cos(angle), np.sin(angle)], axis=0)
        forward.append(split_bf16(table))
        inverse.append(split_bf16(np.ascontiguousarray(table.T)))
    return np.stack(forward), np.stack(inverse)


def split_value(values):
    high = values.astype(jnp.bfloat16)
    low = (values - high.astype(jnp.float32)).astype(jnp.bfloat16)
    return high, low


def matmul(a, b):
    return jnp.dot(a, b, preferred_element_type=jnp.float32)


def exact_matmul(table, data):
    return matmul(table, jnp.concatenate([data, data], axis=0))


def split_matmul(table, high, low):
    return exact_matmul(table, high) + matmul(table[:, : table.shape[1] // 2], low)


def butterfly(even, odd, rows, cols, half_len):
    sin_rows = slice(half_len + rows.start, half_len + rows.stop)
    even_cos, odd_cos = even[rows, cols], odd[rows, cols]
    even_sin, odd_sin = even[sin_rows, cols], odd[sin_rows, cols]
    return (
        (even_cos + odd_cos, even_sin + odd_sin),
        (even_cos - odd_cos, odd_sin - even_sin),
    )


def store_product(ref, rows, cols, half_len, lower, upper):
    sin_rows = slice(half_len + rows.start, half_len + rows.stop)
    values = (
        (0, rows, lower[0] + upper[0]),
        (0, sin_rows, lower[1] - upper[1]),
        (1, rows, lower[0] - upper[0]),
        (1, sin_rows, lower[1] + upper[1]),
    )
    for parity, to_rows, value in values:
        high, low = split_value(value)
        ref[parity, 0, to_rows, cols] = high
        ref[parity, 1, to_rows, cols] = low


def times(a, b):
    return a[0] * b[0] - a[1] * b[1], a[0] * b[1] + a[1] * b[0]


def times_conj(a, b):
    return a[0] * b[0] + a[1] * b[1], a[1] * b[0] - a[0] * b[1]


def partner(me, distance, n):
    total, bit = 0, 1
    while bit < n:
        digit = lax.rem(me // bit, 2)
        total = total + bit * (1 - digit if distance & bit else digit)
        bit *= 2
    return total


def fused_kernel(
    n,
    key_hbm, value_hbm, ograd_hbm, query_hbm, filt_hbm, fwd_hbm, inv_hbm,
    back, fg_hbm,
    key, value, ograd, query, filt, fwd, inv,
    stage, send, arrived, filt_t, filt_spec, spec, prod, cross, joined, result, fg,
    load_sem, store_sem, send_sem, recv_sem,
):
    rows, channels = key.shape
    per_group, length = filt.shape
    width = per_group // HALVES
    scale = 1.0 / (length * math.sqrt(length))
    me = lax.axis_index("seq")
    others = list(range(n - 1, 0, -1))

    loads = [
        pltpu.make_async_copy(src, dst, load_sem.at[i])
        for i, (src, dst) in enumerate(
            [
                (key_hbm, key),
                (value_hbm, value),
                (ograd_hbm, ograd),
                (query_hbm, query),
                (filt_hbm, filt),
                (fwd_hbm, fwd),
                (inv_hbm, inv),
            ]
        )
    ]
    for load in loads[:4]:
        load.start()
    barrier = pltpu.get_barrier_semaphore()
    for d in others:
        pl.semaphore_signal(
            barrier, inc=1, device_id={"seq": partner(me, d, n)}, device_id_type=MESH
        )
    for load in loads[:4]:
        load.wait()
    for load in loads[4:]:
        load.start()

    def columns(owner, half):
        return pl.ds(pl.multiple_of(owner * per_group + half * width, width), width)

    def row_block(owner):
        return pl.ds(pl.multiple_of(owner * rows, rows), rows)

    def gates(half, owner):
        cols = columns(owner, half)
        mixed = key[:, cols].astype(jnp.float32) * value[:, cols].astype(jnp.float32)
        gated = ograd[:, cols].astype(jnp.float32) * query[:, cols].astype(jnp.float32)
        return mixed.astype(jnp.bfloat16), gated.astype(jnp.bfloat16)

    half_len, half_rows = length // 2, rows // 2

    def parity_rows(parity, count):
        return pl.ds(parity, count, stride=2)

    def split_rows(half, owner, slot):
        mixed, gated = gates(half, owner)
        stage[slot, 0] = mixed.astype(jnp.float32)
        stage[slot, 1] = gated.astype(jnp.float32)
        return [
            [stage[slot, i, parity_rows(parity, half_rows), :].astype(jnp.bfloat16) for i in range(2)]
            for parity in range(2)
        ]

    def half_block(owner):
        return pl.ds(pl.multiple_of(owner * half_rows, half_rows), half_rows)

    def fill(half, d):
        for parity, pair in enumerate(split_rows(half, partner(me, d, n), d)):
            send[half, d, parity, :, :width] = pair[0]
            send[half, d, parity, :, width:] = pair[1]

    def out_copy(half, d):
        return pltpu.make_async_remote_copy(
            src_ref=send.at[half, d],
            dst_ref=arrived.at[half, :, half_block(me)],
            send_sem=send_sem.at[0, half, d],
            recv_sem=recv_sem.at[0, half, d],
            device_id={"seq": partner(me, d, n)},
            device_id_type=MESH,
        )

    def back_copy(half, d):
        return pltpu.make_async_remote_copy(
            src_ref=result.at[half, row_block(partner(me, d, n))],
            dst_ref=back.at[half, me],
            send_sem=send_sem.at[1, half, d],
            recv_sem=recv_sem.at[1, half, d],
            device_id={"seq": partner(me, d, n)},
            device_id_type=MESH,
        )

    for d in others:
        fill(0, d)
    pl.semaphore_wait(barrier, n - 1)
    sent = {}
    for half in range(HALVES):
        for d in others:
            if half > 0:
                fill(half, d)
            sent[0, half, d] = out_copy(half, d)
            sent[0, half, d].start()
    for half in range(HALVES):
        for parity, pair in enumerate(split_rows(half, me, 0)):
            arrived[half, parity, half_block(me), :width] = pair[0]
            arrived[half, parity, half_block(me), width:] = pair[1]

    loads[4].wait()
    for i in range(HALVES):
        filt_t[i] = filt[i * width : (i + 1) * width, :].T
    loads[5].wait()
    every = slice(0, per_group)
    for parity in range(2):
        rows_now = parity_rows(parity, half_len)
        high, low = split_value(
            jnp.concatenate([filt_t[i, rows_now, :] for i in range(HALVES)], axis=1)
        )
        spec[0, parity] = split_matmul(fwd[parity], high, low)
    chunk = min(64, half_len)
    chunks = [slice(start, start + chunk) for start in range(0, half_len, chunk)]
    for part in chunks:
        for upper, pair in enumerate(butterfly(spec.at[0, 0], spec.at[0, 1], part, every, half_len)):
            for which in range(2):
                filt_spec[upper, which, part] = pair[which]
    loads[6].wait()

    left, right = slice(0, width), slice(width, 2 * width)

    def inverse_join(products):
        for parity in range(2):
            out = split_matmul(inv[parity], products[parity, 0], products[parity, 1])
            for i in range(2):
                joined[i, parity_rows(parity, half_len), :] = (
                    out[:, i * width : (i + 1) * width] * scale
                )

    own = []
    for half in range(HALVES):
        for d in others:
            sent[0, half, d].wait_recv()
        for parity in range(2):
            spec[half, parity] = exact_matmul(fwd[parity], arrived[half, parity])
        even, odd = spec.at[half, 0], spec.at[half, 1]
        fcols = slice(half * width, (half + 1) * width)
        for part in chunks:
            mixed = butterfly(even, odd, part, left, half_len)
            gated = butterfly(even, odd, part, right, half_len)
            taps = [
                (filt_spec[upper, 0, part, fcols], filt_spec[upper, 1, part, fcols])
                for upper in range(2)
            ]
            store_product(
                prod, part, left, half_len, times(mixed[0], taps[0]), times(mixed[1], taps[1])
            )
            store_product(
                prod, part, right, half_len,
                times_conj(gated[0], taps[0]), times_conj(gated[1], taps[1]),
            )
        inverse_join(prod)
        result[half, :, :width] = joined[0].astype(jnp.bfloat16)
        result[half, :, width:] = joined[1].astype(jnp.bfloat16)
        for d in others:
            sent[1, half, d] = back_copy(half, d)
            sent[1, half, d].start()
        own.append(
            pltpu.make_async_copy(
                result.at[half, row_block(me)], back.at[half, me], store_sem.at[1 + half]
            )
        )
        own[-1].start()

    for half in range(HALVES):
        even, odd = spec.at[half, 0], spec.at[half, 1]
        fcols = slice(half * width, (half + 1) * width)
        for part in chunks:
            mixed = butterfly(even, odd, part, left, half_len)
            gated = butterfly(even, odd, part, right, half_len)
            store_product(
                cross, part, fcols, half_len,
                times_conj(gated[0], mixed[0]), times_conj(gated[1], mixed[1]),
            )
    inverse_join(cross)
    for i in range(HALVES):
        fg[i * width : (i + 1) * width, :] = joined[i].T
    store_fg = pltpu.make_async_copy(fg, fg_hbm, store_sem.at[0])
    store_fg.start()

    for half in range(HALVES):
        for d in others:
            sent[1, half, d].wait_recv()
    for copy in sent.values():
        copy.wait_send()
    for store in own + [store_fg]:
        store.wait()


def gate_kernel(
    key_hbm, value_hbm, ograd_hbm, back_hbm, fg_in, gq_hbm, gk_hbm, gv_hbm, fg_out,
    key, value, ograd, back, gq, gk, gv, fg, load_sem, store_sem,
):
    pieces, n, rows, double = back.shape
    width = double // 2
    load_fg = pltpu.make_async_copy(fg_in, fg, load_sem.at[0, 4])
    store_fg = pltpu.make_async_copy(fg, fg_out, store_sem.at[0, 0])
    block = rows // GATE_STEPS
    loads = []
    for step in range(GATE_STEPS):
        part = pl.ds(step * block, block)
        pairs = [
            (back_hbm.at[:, :, part], back.at[:, :, part]),
            (key_hbm.at[part], key.at[part]),
            (value_hbm.at[part], value.at[part]),
            (ograd_hbm.at[part], ograd.at[part]),
        ]
        loads.append(
            [pltpu.make_async_copy(s, d, load_sem.at[step, i]) for i, (s, d) in enumerate(pairs)]
        )
        for load in loads[-1]:
            load.start()
        if step == 0:
            load_fg.start()
    stores = [store_fg]
    for step in range(GATE_STEPS):
        part = pl.ds(step * block, block)
        for load in loads[step]:
            load.wait()
        for owner in range(n):
            for half in range(pieces):
                first = (owner * pieces + half) * width
                cols = slice(first, first + width)
                conv = back[half, owner, part, :width].astype(jnp.float32)
                igrad = back[half, owner, part, width:].astype(jnp.float32)
                gq[part, cols] = (ograd[part, cols].astype(jnp.float32) * conv).astype(gq.dtype)
                gk[part, cols] = (value[part, cols].astype(jnp.float32) * igrad).astype(gk.dtype)
                gv[part, cols] = (key[part, cols].astype(jnp.float32) * igrad).astype(gv.dtype)
        for i, (src, dst) in enumerate([(gq, gq_hbm), (gk, gk_hbm), (gv, gv_hbm)]):
            store = pltpu.make_async_copy(src.at[part], dst.at[part], store_sem.at[step, 1 + i])
            store.start()
            stores.append(store)
        if step == 0:
            load_fg.wait()
            store_fg.start()
    for store in stores:
        store.wait()


def fused(query, key_in, value, out_grad, filters):
    n = lax.axis_size("seq")
    rows, channels = query.shape
    per_group, length = filters.shape
    width = per_group // HALVES
    forward, inverse = dft_tables(length)
    bf16, f32 = jnp.bfloat16, jnp.float32
    gate = pltpu.VMEM((rows, channels), bf16)
    gate_shape = jax.ShapeDtypeStruct((rows, channels), bf16)
    back_shape = (HALVES, n, rows, 2 * width)
    fg_shape = jax.ShapeDtypeStruct((per_group, length), f32)
    any_space = pl.BlockSpec(memory_space=pl.ANY)
    hbm = pl.BlockSpec(memory_space=pltpu.HBM)
    back, filter_grad = pl.pallas_call(
        functools.partial(fused_kernel, n),
        out_shape=(jax.ShapeDtypeStruct(back_shape, bf16), fg_shape),
        in_specs=[hbm] * 7,
        out_specs=(any_space,) * 2,
        scratch_shapes=[
            gate, gate, gate, gate,
            pltpu.VMEM((per_group, length), f32),
            pltpu.VMEM(forward.shape, bf16),
            pltpu.VMEM(inverse.shape, bf16),
            pltpu.VMEM((n, 2, rows, width), f32),
            pltpu.VMEM((HALVES, n, 2, rows // 2, 2 * width), bf16),
            pltpu.VMEM((HALVES, 2, length // 2, 2 * width), bf16),
            pltpu.VMEM((HALVES, length, width), f32),
            pltpu.VMEM((2, 2, length // 2, per_group), f32),
            pltpu.VMEM((HALVES, 2, length, 2 * width), f32),
            pltpu.VMEM((2, 2, length, 2 * width), bf16),
            pltpu.VMEM((2, 2, length, per_group), bf16),
            pltpu.VMEM((HALVES, length, width), f32),
            pltpu.VMEM((HALVES, length, 2 * width), bf16),
            pltpu.VMEM((per_group, length), f32),
            pltpu.SemaphoreType.DMA((7,)),
            pltpu.SemaphoreType.DMA((1 + HALVES,)),
            pltpu.SemaphoreType.DMA((2, HALVES, n)),
            pltpu.SemaphoreType.DMA((2, HALVES, n)),
        ],
        compiler_params=pltpu.CompilerParams(
            collective_id=0, has_side_effects=True, vmem_limit_bytes=VMEM_BYTES
        ),
        cost_estimate=pl.CostEstimate(
            flops=2 * 16 * 2 * length * length * per_group,
            bytes_accessed=12 * 1024 * 1024,
            transcendentals=0,
        ),
        name="hyena_bwd",
    )(key_in, value, out_grad, query, filters, jnp.asarray(forward), jnp.asarray(inverse))
    return pl.pallas_call(
        gate_kernel,
        out_shape=(gate_shape, gate_shape, gate_shape, fg_shape),
        in_specs=[hbm] * 3 + [any_space] * 2,
        out_specs=(hbm,) * 4,
        scratch_shapes=[
            gate, gate, gate,
            pltpu.VMEM(back_shape, bf16),
            gate, gate, gate,
            pltpu.VMEM((per_group, length), f32),
            pltpu.SemaphoreType.DMA((GATE_STEPS, 5)),
            pltpu.SemaphoreType.DMA((GATE_STEPS, 4)),
        ],
        compiler_params=pltpu.CompilerParams(vmem_limit_bytes=VMEM_BYTES),
        cost_estimate=pl.CostEstimate(
            flops=6 * rows * channels, bytes_accessed=4 * 1024 * 1024, transcendentals=0
        ),
        name="output_gates",
    )(key_in, value, out_grad, back, filter_grad)


def twiddle_tables(rows, cols, modulus, direction):
    row_index = lax.broadcasted_iota(jnp.int32, (rows, cols), 0)
    col_index = lax.broadcasted_iota(jnp.int32, (rows, cols), 1)
    angles = (
        direction * 2.0 * math.pi * (row_index * col_index % modulus).astype(jnp.float32) / modulus
    )
    return (jnp.cos(angles), jnp.sin(angles))


def complex_apply(real_part, imag_part, cosine, sines, form):
    highest = lax.Precision.HIGHEST
    out_real = jnp.einsum(form, real_part, cosine, precision=highest) - jnp.einsum(
        form, imag_part, sines, precision=highest
    )
    out_imag = jnp.einsum(form, real_part, sines, precision=highest) + jnp.einsum(
        form, imag_part, cosine, precision=highest
    )
    return (out_real, out_imag)


def transform(real_part, imag_part, direction):
    length = real_part.shape[-1]
    radix_one = math.gcd(length, 128)
    if length <= 256 or radix_one == 1:
        cosine, sines = twiddle_tables(length, length, length, direction)
        return complex_apply(real_part, imag_part, cosine, sines, "...j,kj->...k")
    radix_two = length // radix_one
    leading = real_part.shape[:-1]
    real_part = real_part.reshape(leading + (radix_one, radix_two))
    imag_part = imag_part.reshape(leading + (radix_one, radix_two))
    cosine, sines = twiddle_tables(radix_one, radix_one, radix_one, direction)
    real_part, imag_part = complex_apply(real_part, imag_part, cosine, sines, "...jm,kj->...km")
    cosine, sines = twiddle_tables(radix_one, radix_two, length, direction)
    real_part, imag_part = (
        real_part * cosine - imag_part * sines,
        real_part * sines + imag_part * cosine,
    )
    real_part, imag_part = transform(real_part, imag_part, direction)
    real_part = jnp.swapaxes(real_part, -1, -2).reshape(leading + (length,))
    imag_part = jnp.swapaxes(imag_part, -1, -2).reshape(leading + (length,))
    return (real_part, imag_part)


def mirrored(values):
    return jnp.roll(jnp.flip(values, -1), 1, -1)


def filter_work(mixed_part, gated_part, own_filter):
    length = mixed_part.shape[-1]
    padded_len = 2 * length
    factor = 1.0 / math.sqrt(length)

    def padded(values):
        widths = [(0, 0)] * (values.ndim - 1) + [(0, length)]
        return jnp.pad(values.astype(jnp.float32), widths)

    def inverse(real_part, imag_part):
        out_real, out_imag = transform(real_part, imag_part, 1.0)
        scale = factor / padded_len
        return (out_real[..., :length] * scale, out_imag[..., :length] * scale)

    both_re, both_im = transform(padded(mixed_part), padded(gated_part), -1.0)
    mirror_re, mirror_im = (mirrored(both_re), mirrored(both_im))
    mix_re = 0.5 * (both_re + mirror_re)
    mix_im = 0.5 * (both_im - mirror_im)
    gate_re = 0.5 * (both_im + mirror_im)
    gate_im = -0.5 * (both_re - mirror_re)
    filt_pad = padded(own_filter)
    filt_re, filt_im = transform(filt_pad, jnp.zeros_like(filt_pad), -1.0)
    conv_re = mix_re * filt_re - mix_im * filt_im
    conv_im = mix_re * filt_im + mix_im * filt_re
    back_re = gate_re * filt_re + gate_im * filt_im
    back_im = gate_im * filt_re - gate_re * filt_im
    conv_out, input_grad = inverse(conv_re - back_im, conv_im + back_re)
    filter_grad, unused = inverse(
        gate_re * mix_re + gate_im * mix_im, gate_im * mix_re - gate_re * mix_im
    )
    return (conv_out.astype(jnp.bfloat16), input_grad.astype(jnp.bfloat16), filter_grad)


def on_device(query, key_in, value, out_grad, filters):
    tok_rows, channels = query.shape
    groups = lax.axis_size("seq")
    per_group = channels // groups
    if groups & (groups - 1) == 0 and filters.shape[1] <= 1024 and per_group == 128 * HALVES and tok_rows % 32 == 0:
        return fused(query, key_in, value, out_grad, filters)
    mixed = (key_in.astype(jnp.float32) * value.astype(jnp.float32)).astype(jnp.bfloat16)
    gated = (out_grad.astype(jnp.float32) * query.astype(jnp.float32)).astype(jnp.bfloat16)
    send_mixed = mixed.T.reshape(groups, per_group, tok_rows)
    send_gated = gated.T.reshape(groups, per_group, tok_rows)
    own_filter = filters[None]
    arrived_mix, arrived_gate = (
        lax.all_to_all(send_mixed, "seq", split_axis=0, concat_axis=2, tiled=True),
        lax.all_to_all(send_gated, "seq", split_axis=0, concat_axis=2, tiled=True),
    )
    conv_out, input_grad, filter_grad = filter_work(arrived_mix, arrived_gate, own_filter)
    back_conv, back_grad = (
        lax.all_to_all(conv_out, "seq", split_axis=2, concat_axis=0, tiled=True),
        lax.all_to_all(input_grad, "seq", split_axis=2, concat_axis=0, tiled=True),
    )
    back_conv = back_conv.reshape(channels, tok_rows).T
    back_grad = back_grad.reshape(channels, tok_rows).T
    grad_query = (out_grad.astype(jnp.float32) * back_conv.astype(jnp.float32)).astype(jnp.bfloat16)
    grad_key = (back_grad.astype(jnp.float32) * value.astype(jnp.float32)).astype(jnp.bfloat16)
    grad_value = (back_grad.astype(jnp.float32) * key_in.astype(jnp.float32)).astype(jnp.bfloat16)
    return (grad_query, grad_key, grad_value, filter_grad[0])


def solution(mesh):
    placed = (
        P("seq", "ch"),
        P("seq", "ch"),
        P("seq", "ch"),
        P("seq", "ch"),
        P(("ch", "seq"), None),
    )
    return jax.shard_map(
        on_device,
        mesh=mesh,
        in_specs=placed,
        out_specs=(P("seq", "ch"), P("seq", "ch"), P("seq", "ch"), P(("ch", "seq"), None)),
        check_vma=False,
    )
```

```python
import functools
import math

import jax
import jax.numpy as jnp
import ml_dtypes
import numpy as np
from jax import lax
from jax.experimental import pallas as pl
from jax.experimental.pallas import tpu as pltpu
from jax.sharding import PartitionSpec as P

HALVES = 2
GATE_STEPS = 2
VMEM_BYTES = 63 * 1024 * 1024
MESH = pl.DeviceIdType.MESH


def split_bf16(table):
    high = table.astype(ml_dtypes.bfloat16)
    low = (table - high.astype(np.float64)).astype(ml_dtypes.bfloat16)
    return np.concatenate([high, low], axis=1)


def dft_tables(length):
    freq = 2 * np.arange(length // 2)[:, None] + 1
    forward, inverse = [], []
    for parity in range(2):
        time = np.arange(parity, length, 2)[None, :]
        angle = np.pi * ((freq * time) % (4 * length)) / (2 * length)
        table = np.concatenate([np.cos(angle), np.sin(angle)], axis=0)
        forward.append(split_bf16(table))
        inverse.append(split_bf16(np.ascontiguousarray(table.T)))
    return np.stack(forward), np.stack(inverse)


def split_value(values):
    high = values.astype(jnp.bfloat16)
    low = (values - high.astype(jnp.float32)).astype(jnp.bfloat16)
    return high, low


def matmul(a, b):
    return jnp.dot(a, b, preferred_element_type=jnp.float32)


def exact_matmul(table, data):
    return matmul(table, jnp.concatenate([data, data], axis=0))


def split_matmul(table, high, low):
    return exact_matmul(table, high) + matmul(table[:, : table.shape[1] // 2], low)


def butterfly(even, odd, rows, cols, half_len):
    sin_rows = slice(half_len + rows.start, half_len + rows.stop)
    even_cos, odd_cos = even[rows, cols], odd[rows, cols]
    even_sin, odd_sin = even[sin_rows, cols], odd[sin_rows, cols]
    return (
        (even_cos + odd_cos, even_sin + odd_sin),
        (even_cos - odd_cos, odd_sin - even_sin),
    )


def store_product(ref, rows, cols, half_len, lower, upper):
    sin_rows = slice(half_len + rows.start, half_len + rows.stop)
    values = (
        (0, rows, lower[0] + upper[0]),
        (0, sin_rows, lower[1] - upper[1]),
        (1, rows, lower[0] - upper[0]),
        (1, sin_rows, lower[1] + upper[1]),
    )
    for parity, to_rows, value in values:
        high, low = split_value(value)
        ref[parity, 0, to_rows, cols] = high
        ref[parity, 1, to_rows, cols] = low


def times(a, b):
    return a[0] * b[0] - a[1] * b[1], a[0] * b[1] + a[1] * b[0]


def times_conj(a, b):
    return a[0] * b[0] + a[1] * b[1], a[1] * b[0] - a[0] * b[1]


def partner(me, distance, n):
    total, bit = 0, 1
    while bit < n:
        digit = lax.rem(me // bit, 2)
        total = total + bit * (1 - digit if distance & bit else digit)
        bit *= 2
    return total


def fused_kernel(
    n,
    key_hbm, value_hbm, ograd_hbm, query_hbm, filt_hbm, fwd_hbm, inv_hbm,
    back, fg_hbm,
    key, value, ograd, query, filt, fwd, inv,
    stage, send, arrived, filt_t, filt_raw, filt_spec, spec, prod, cross, joined, result, fg,
    load_sem, store_sem, send_sem, recv_sem,
):
    rows, channels = key.shape
    per_group, length = filt.shape
    width = per_group // HALVES
    scale = 1.0 / (length * math.sqrt(length))
    me = lax.axis_index("seq")
    others = list(range(n - 1, 0, -1))

    loads = [
        pltpu.make_async_copy(src, dst, load_sem.at[i])
        for i, (src, dst) in enumerate(
            [
                (key_hbm, key),
                (value_hbm, value),
                (ograd_hbm, ograd),
                (query_hbm, query),
                (filt_hbm, filt),
                (fwd_hbm, fwd),
                (inv_hbm, inv),
            ]
        )
    ]
    for load in loads[:4]:
        load.start()
    barrier = pltpu.get_barrier_semaphore()
    for d in others:
        pl.semaphore_signal(
            barrier, inc=1, device_id={"seq": partner(me, d, n)}, device_id_type=MESH
        )

    def columns(owner, half):
        return pl.ds(pl.multiple_of(owner * per_group + half * width, width), width)

    def row_block(owner):
        return pl.ds(pl.multiple_of(owner * rows, rows), rows)

    def gate(piece, owner):
        cols = columns(owner, piece // 2)
        one, two = (ograd, query) if piece % 2 else (key, value)
        return one[:, cols].astype(jnp.float32) * two[:, cols].astype(jnp.float32)

    half_len, half_rows = length // 2, rows // 2

    def parity_rows(parity, count):
        return pl.ds(parity, count, stride=2)

    def split_rows(piece, owner, slot):
        stage[slot] = gate(piece, owner).astype(jnp.bfloat16).astype(jnp.float32)
        return [
            stage[slot, parity_rows(parity, half_rows), :].astype(jnp.bfloat16)
            for parity in range(2)
        ]

    def half_block(owner):
        return pl.ds(pl.multiple_of(owner * half_rows, half_rows), half_rows)

    def fill(piece, d):
        for parity, values in enumerate(split_rows(piece, partner(me, d, n), d)):
            send[piece, d, parity] = values

    def out_copy(piece, d):
        return pltpu.make_async_remote_copy(
            src_ref=send.at[piece, d],
            dst_ref=arrived.at[piece, :, half_block(me)],
            send_sem=send_sem.at[0, piece, d],
            recv_sem=recv_sem.at[0, piece, d],
            device_id={"seq": partner(me, d, n)},
            device_id_type=MESH,
        )

    def back_copy(piece, d):
        return pltpu.make_async_remote_copy(
            src_ref=result.at[piece, row_block(partner(me, d, n))],
            dst_ref=back.at[piece, me],
            send_sem=send_sem.at[1, piece, d],
            recv_sem=recv_sem.at[1, piece, d],
            device_id={"seq": partner(me, d, n)},
            device_id_type=MESH,
        )

    pieces = range(2 * HALVES)
    sent = {}
    for piece in pieces:
        if piece < 2:
            loads[2 * piece].wait()
            loads[2 * piece + 1].wait()
        for d in others:
            fill(piece, d)
            if piece == 0 and d == others[-1]:
                pl.semaphore_wait(barrier, n - 1)
                for e in others:
                    sent[0, 0, e] = out_copy(0, e)
                    sent[0, 0, e].start()
            elif piece > 0:
                sent[0, piece, d] = out_copy(piece, d)
                sent[0, piece, d].start()
    for load in loads[4:]:
        load.start()
    for piece in pieces:
        for parity, values in enumerate(split_rows(piece, me, 0)):
            arrived[piece, parity, half_block(me)] = values

    loads[4].wait()
    for i in range(HALVES):
        filt_t[i] = filt[i * width : (i + 1) * width, :].T
    loads[5].wait()
    every = slice(0, per_group)
    for parity in range(2):
        rows_now = parity_rows(parity, half_len)
        high, low = split_value(
            jnp.concatenate([filt_t[i, rows_now, :] for i in range(HALVES)], axis=1)
        )
        filt_raw[parity] = split_matmul(fwd[parity], high, low)
    chunk = min(64, half_len)
    chunks = [slice(start, start + chunk) for start in range(0, half_len, chunk)]
    for part in chunks:
        for upper, pair in enumerate(butterfly(filt_raw.at[0], filt_raw.at[1], part, every, half_len)):
            for which in range(2):
                filt_spec[upper, which, part] = pair[which]
    loads[6].wait()

    def inverse_join(products):
        for parity in range(2):
            out = split_matmul(inv[parity], products[parity, 0], products[parity, 1])
            for i in range(out.shape[1] // width):
                joined[i, parity_rows(parity, half_len), :] = (
                    out[:, i * width : (i + 1) * width] * scale
                )

    every = slice(0, width)
    own = []
    for piece in pieces:
        for d in others:
            sent[0, piece, d].wait_recv()
        for parity in range(2):
            spec[piece, parity] = exact_matmul(fwd[parity], arrived[piece, parity])
        even, odd = spec.at[piece, 0], spec.at[piece, 1]
        fcols = slice((piece // 2) * width, (piece // 2 + 1) * width)
        multiply = times_conj if piece % 2 else times
        for part in chunks:
            data = butterfly(even, odd, part, every, half_len)
            lower, upper = [
                multiply(data[i], (filt_spec[i, 0, part, fcols], filt_spec[i, 1, part, fcols]))
                for i in range(2)
            ]
            store_product(prod, part, every, half_len, lower, upper)
        inverse_join(prod)
        result[piece] = joined[0].astype(jnp.bfloat16)
        for d in others:
            sent[1, piece, d] = back_copy(piece, d)
            sent[1, piece, d].start()
        own.append(
            pltpu.make_async_copy(
                result.at[piece, row_block(me)], back.at[piece, me], store_sem.at[1 + piece]
            )
        )
        own[-1].start()

    for half in range(HALVES):
        fcols = slice(half * width, (half + 1) * width)
        for part in chunks:
            mixed, gated = [
                butterfly(spec.at[piece, 0], spec.at[piece, 1], part, every, half_len)
                for piece in (2 * half, 2 * half + 1)
            ]
            store_product(
                cross, part, fcols, half_len,
                times_conj(gated[0], mixed[0]), times_conj(gated[1], mixed[1]),
            )
    inverse_join(cross)
    for i in range(HALVES):
        fg[i * width : (i + 1) * width, :] = joined[i].T
    store_fg = pltpu.make_async_copy(fg, fg_hbm, store_sem.at[0])
    store_fg.start()

    for piece in pieces:
        for d in others:
            sent[1, piece, d].wait_recv()
    for copy in sent.values():
        copy.wait_send()
    for store in own + [store_fg]:
        store.wait()


def gate_kernel(
    key_hbm, value_hbm, ograd_hbm, back_hbm, fg_in, gq_hbm, gk_hbm, gv_hbm, fg_out,
    key, value, ograd, back, gq, gk, gv, fg, load_sem, store_sem,
):
    pieces, n, rows, width = back.shape
    halves = pieces // 2
    load_fg = pltpu.make_async_copy(fg_in, fg, load_sem.at[0, 4])
    store_fg = pltpu.make_async_copy(fg, fg_out, store_sem.at[0, 0])
    block = rows // GATE_STEPS
    loads = []
    for step in range(GATE_STEPS):
        part = pl.ds(step * block, block)
        pairs = [
            (back_hbm.at[:, :, part], back.at[:, :, part]),
            (key_hbm.at[part], key.at[part]),
            (value_hbm.at[part], value.at[part]),
            (ograd_hbm.at[part], ograd.at[part]),
        ]
        loads.append(
            [pltpu.make_async_copy(s, d, load_sem.at[step, i]) for i, (s, d) in enumerate(pairs)]
        )
        for load in loads[-1]:
            load.start()
        if step == 0:
            load_fg.start()
    stores = [store_fg]
    for step in range(GATE_STEPS):
        part = pl.ds(step * block, block)
        for load in loads[step]:
            load.wait()
        for owner in range(n):
            for half in range(halves):
                first = (owner * halves + half) * width
                cols = slice(first, first + width)
                conv = back[2 * half, owner, part].astype(jnp.float32)
                igrad = back[2 * half + 1, owner, part].astype(jnp.float32)
                gq[part, cols] = (ograd[part, cols].astype(jnp.float32) * conv).astype(gq.dtype)
                gk[part, cols] = (value[part, cols].astype(jnp.float32) * igrad).astype(gk.dtype)
                gv[part, cols] = (key[part, cols].astype(jnp.float32) * igrad).astype(gv.dtype)
        for i, (src, dst) in enumerate([(gq, gq_hbm), (gk, gk_hbm), (gv, gv_hbm)]):
            store = pltpu.make_async_copy(src.at[part], dst.at[part], store_sem.at[step, 1 + i])
            store.start()
            stores.append(store)
        if step == 0:
            load_fg.wait()
            store_fg.start()
    for store in stores:
        store.wait()


def fused(query, key_in, value, out_grad, filters):
    n = lax.axis_size("seq")
    rows, channels = query.shape
    per_group, length = filters.shape
    width = per_group // HALVES
    forward, inverse = dft_tables(length)
    bf16, f32 = jnp.bfloat16, jnp.float32
    gate = pltpu.VMEM((rows, channels), bf16)
    gate_shape = jax.ShapeDtypeStruct((rows, channels), bf16)
    back_shape = (2 * HALVES, n, rows, width)
    fg_shape = jax.ShapeDtypeStruct((per_group, length), f32)
    any_space = pl.BlockSpec(memory_space=pl.ANY)
    hbm = pl.BlockSpec(memory_space=pltpu.HBM)
    back, filter_grad = pl.pallas_call(
        functools.partial(fused_kernel, n),
        out_shape=(jax.ShapeDtypeStruct(back_shape, bf16), fg_shape),
        in_specs=[hbm] * 7,
        out_specs=(any_space,) * 2,
        scratch_shapes=[
            gate, gate, gate, gate,
            pltpu.VMEM((per_group, length), f32),
            pltpu.VMEM(forward.shape, bf16),
            pltpu.VMEM(inverse.shape, bf16),
            pltpu.VMEM((n, rows, width), f32),
            pltpu.VMEM((2 * HALVES, n, 2, rows // 2, width), bf16),
            pltpu.VMEM((2 * HALVES, 2, length // 2, width), bf16),
            pltpu.VMEM((HALVES, length, width), f32),
            pltpu.VMEM((2, length, per_group), f32),
            pltpu.VMEM((2, 2, length // 2, per_group), f32),
            pltpu.VMEM((2 * HALVES, 2, length, width), f32),
            pltpu.VMEM((2, 2, length, width), bf16),
            pltpu.VMEM((2, 2, length, per_group), bf16),
            pltpu.VMEM((HALVES, length, width), f32),
            pltpu.VMEM((2 * HALVES, length, width), bf16),
            pltpu.VMEM((per_group, length), f32),
            pltpu.SemaphoreType.DMA((7,)),
            pltpu.SemaphoreType.DMA((1 + 2 * HALVES,)),
            pltpu.SemaphoreType.DMA((2, 2 * HALVES, n)),
            pltpu.SemaphoreType.DMA((2, 2 * HALVES, n)),
        ],
        compiler_params=pltpu.CompilerParams(
            collective_id=0, has_side_effects=True, vmem_limit_bytes=VMEM_BYTES
        ),
        cost_estimate=pl.CostEstimate(
            flops=2 * 16 * 2 * length * length * per_group,
            bytes_accessed=12 * 1024 * 1024,
            transcendentals=0,
        ),
        name="hyena_bwd",
    )(key_in, value, out_grad, query, filters, jnp.asarray(forward), jnp.asarray(inverse))
    return pl.pallas_call(
        gate_kernel,
        out_shape=(gate_shape, gate_shape, gate_shape, fg_shape),
        in_specs=[hbm] * 3 + [any_space] * 2,
        out_specs=(hbm,) * 4,
        scratch_shapes=[
            gate, gate, gate,
            pltpu.VMEM(back_shape, bf16),
            gate, gate, gate,
            pltpu.VMEM((per_group, length), f32),
            pltpu.SemaphoreType.DMA((GATE_STEPS, 5)),
            pltpu.SemaphoreType.DMA((GATE_STEPS, 4)),
        ],
        compiler_params=pltpu.CompilerParams(vmem_limit_bytes=VMEM_BYTES),
        cost_estimate=pl.CostEstimate(
            flops=6 * rows * channels, bytes_accessed=4 * 1024 * 1024, transcendentals=0
        ),
        name="output_gates",
    )(key_in, value, out_grad, back, filter_grad)


def twiddle_tables(rows, cols, modulus, direction):
    row_index = lax.broadcasted_iota(jnp.int32, (rows, cols), 0)
    col_index = lax.broadcasted_iota(jnp.int32, (rows, cols), 1)
    angles = (
        direction * 2.0 * math.pi * (row_index * col_index % modulus).astype(jnp.float32) / modulus
    )
    return (jnp.cos(angles), jnp.sin(angles))


def complex_apply(real_part, imag_part, cosine, sines, form):
    highest = lax.Precision.HIGHEST
    out_real = jnp.einsum(form, real_part, cosine, precision=highest) - jnp.einsum(
        form, imag_part, sines, precision=highest
    )
    out_imag = jnp.einsum(form, real_part, sines, precision=highest) + jnp.einsum(
        form, imag_part, cosine, precision=highest
    )
    return (out_real, out_imag)


def transform(real_part, imag_part, direction):
    length = real_part.shape[-1]
    radix_one = math.gcd(length, 128)
    if length <= 256 or radix_one == 1:
        cosine, sines = twiddle_tables(length, length, length, direction)
        return complex_apply(real_part, imag_part, cosine, sines, "...j,kj->...k")
    radix_two = length // radix_one
    leading = real_part.shape[:-1]
    real_part = real_part.reshape(leading + (radix_one, radix_two))
    imag_part = imag_part.reshape(leading + (radix_one, radix_two))
    cosine, sines = twiddle_tables(radix_one, radix_one, radix_one, direction)
    real_part, imag_part = complex_apply(real_part, imag_part, cosine, sines, "...jm,kj->...km")
    cosine, sines = twiddle_tables(radix_one, radix_two, length, direction)
    real_part, imag_part = (
        real_part * cosine - imag_part * sines,
        real_part * sines + imag_part * cosine,
    )
    real_part, imag_part = transform(real_part, imag_part, direction)
    real_part = jnp.swapaxes(real_part, -1, -2).reshape(leading + (length,))
    imag_part = jnp.swapaxes(imag_part, -1, -2).reshape(leading + (length,))
    return (real_part, imag_part)


def mirrored(values):
    return jnp.roll(jnp.flip(values, -1), 1, -1)


def filter_work(mixed_part, gated_part, own_filter):
    length = mixed_part.shape[-1]
    padded_len = 2 * length
    factor = 1.0 / math.sqrt(length)

    def padded(values):
        widths = [(0, 0)] * (values.ndim - 1) + [(0, length)]
        return jnp.pad(values.astype(jnp.float32), widths)

    def inverse(real_part, imag_part):
        out_real, out_imag = transform(real_part, imag_part, 1.0)
        scale = factor / padded_len
        return (out_real[..., :length] * scale, out_imag[..., :length] * scale)

    both_re, both_im = transform(padded(mixed_part), padded(gated_part), -1.0)
    mirror_re, mirror_im = (mirrored(both_re), mirrored(both_im))
    mix_re = 0.5 * (both_re + mirror_re)
    mix_im = 0.5 * (both_im - mirror_im)
    gate_re = 0.5 * (both_im + mirror_im)
    gate_im = -0.5 * (both_re - mirror_re)
    filt_pad = padded(own_filter)
    filt_re, filt_im = transform(filt_pad, jnp.zeros_like(filt_pad), -1.0)
    conv_re = mix_re * filt_re - mix_im * filt_im
    conv_im = mix_re * filt_im + mix_im * filt_re
    back_re = gate_re * filt_re + gate_im * filt_im
    back_im = gate_im * filt_re - gate_re * filt_im
    conv_out, input_grad = inverse(conv_re - back_im, conv_im + back_re)
    filter_grad, unused = inverse(
        gate_re * mix_re + gate_im * mix_im, gate_im * mix_re - gate_re * mix_im
    )
    return (conv_out.astype(jnp.bfloat16), input_grad.astype(jnp.bfloat16), filter_grad)


def on_device(query, key_in, value, out_grad, filters):
    tok_rows, channels = query.shape
    groups = lax.axis_size("seq")
    per_group = channels // groups
    if groups & (groups - 1) == 0 and filters.shape[1] <= 1024 and per_group == 128 * HALVES and tok_rows % 32 == 0:
        return fused(query, key_in, value, out_grad, filters)
    mixed = (key_in.astype(jnp.float32) * value.astype(jnp.float32)).astype(jnp.bfloat16)
    gated = (out_grad.astype(jnp.float32) * query.astype(jnp.float32)).astype(jnp.bfloat16)
    send_mixed = mixed.T.reshape(groups, per_group, tok_rows)
    send_gated = gated.T.reshape(groups, per_group, tok_rows)
    own_filter = filters[None]
    arrived_mix, arrived_gate = (
        lax.all_to_all(send_mixed, "seq", split_axis=0, concat_axis=2, tiled=True),
        lax.all_to_all(send_gated, "seq", split_axis=0, concat_axis=2, tiled=True),
    )
    conv_out, input_grad, filter_grad = filter_work(arrived_mix, arrived_gate, own_filter)
    back_conv, back_grad = (
        lax.all_to_all(conv_out, "seq", split_axis=2, concat_axis=0, tiled=True),
        lax.all_to_all(input_grad, "seq", split_axis=2, concat_axis=0, tiled=True),
    )
    back_conv = back_conv.reshape(channels, tok_rows).T
    back_grad = back_grad.reshape(channels, tok_rows).T
    grad_query = (out_grad.astype(jnp.float32) * back_conv.astype(jnp.float32)).astype(jnp.bfloat16)
    grad_key = (back_grad.astype(jnp.float32) * value.astype(jnp.float32)).astype(jnp.bfloat16)
    grad_value = (back_grad.astype(jnp.float32) * key_in.astype(jnp.float32)).astype(jnp.bfloat16)
    return (grad_query, grad_key, grad_value, filter_grad[0])


def solution(mesh):
    placed = (
        P("seq", "ch"),
        P("seq", "ch"),
        P("seq", "ch"),
        P("seq", "ch"),
        P(("ch", "seq"), None),
    )
    return jax.shard_map(
        on_device,
        mesh=mesh,
        in_specs=placed,
        out_specs=(P("seq", "ch"), P("seq", "ch"), P("seq", "ch"), P(("ch", "seq"), None)),
        check_vma=False,
    )
```

```python
import functools
import math

import jax
import jax.numpy as jnp
import ml_dtypes
import numpy as np
from jax import lax
from jax.experimental import pallas as pl
from jax.experimental.pallas import tpu as pltpu
from jax.sharding import PartitionSpec as P

HALVES = 2
GATE_STEPS = 2
VMEM_BYTES = 63 * 1024 * 1024
MESH = pl.DeviceIdType.MESH


def split_bf16(table):
    high = table.astype(ml_dtypes.bfloat16)
    low = (table - high.astype(np.float64)).astype(ml_dtypes.bfloat16)
    return np.concatenate([high, low], axis=1)


def dft_tables(length):
    freq = 2 * np.arange(length // 2)[:, None] + 1
    forward, inverse = [], []
    for parity in range(2):
        time = np.arange(parity, length, 2)[None, :]
        angle = np.pi * ((freq * time) % (4 * length)) / (2 * length)
        table = np.concatenate([np.cos(angle), np.sin(angle)], axis=0)
        forward.append(split_bf16(table))
        inverse.append(split_bf16(np.ascontiguousarray(table.T)))
    return np.stack(forward), np.stack(inverse)


def split_value(values):
    high = values.astype(jnp.bfloat16)
    low = (values - high.astype(jnp.float32)).astype(jnp.bfloat16)
    return high, low


def matmul(a, b):
    return jnp.dot(a, b, preferred_element_type=jnp.float32)


def exact_matmul(table, data):
    return matmul(table, jnp.concatenate([data, data], axis=0))


def split_matmul(table, high, low):
    return exact_matmul(table, high) + matmul(table[:, : table.shape[1] // 2], low)


def butterfly(even, odd, rows, cols, half_len):
    sin_rows = slice(half_len + rows.start, half_len + rows.stop)
    even_cos, odd_cos = even[rows, cols], odd[rows, cols]
    even_sin, odd_sin = even[sin_rows, cols], odd[sin_rows, cols]
    return (
        (even_cos + odd_cos, even_sin + odd_sin),
        (even_cos - odd_cos, odd_sin - even_sin),
    )


def store_product(ref, rows, cols, half_len, lower, upper):
    sin_rows = slice(half_len + rows.start, half_len + rows.stop)
    values = (
        (0, rows, lower[0] + upper[0]),
        (0, sin_rows, lower[1] - upper[1]),
        (1, rows, lower[0] - upper[0]),
        (1, sin_rows, lower[1] + upper[1]),
    )
    for parity, to_rows, value in values:
        high, low = split_value(value)
        ref[parity, 0, to_rows, cols] = high
        ref[parity, 1, to_rows, cols] = low


def times(a, b):
    return a[0] * b[0] - a[1] * b[1], a[0] * b[1] + a[1] * b[0]


def times_conj(a, b):
    return a[0] * b[0] + a[1] * b[1], a[1] * b[0] - a[0] * b[1]


def partner(me, distance, n):
    total, bit = 0, 1
    while bit < n:
        digit = lax.rem(me // bit, 2)
        total = total + bit * (1 - digit if distance & bit else digit)
        bit *= 2
    return total


def fused_kernel(
    n,
    key_hbm, value_hbm, ograd_hbm, query_hbm, filt_hbm, fwd_hbm, inv_hbm,
    back, fg_hbm,
    key, value, ograd, query, filt, fwd, inv,
    stage, send, arrived, filt_t, filt_raw, filt_spec, spec, prod, cross, joined, result, fg,
    load_sem, store_sem, send_sem, recv_sem,
):
    rows, channels = key.shape
    per_group, length = filt.shape
    width = per_group // HALVES
    scale = 1.0 / (length * math.sqrt(length))
    me = lax.axis_index("seq")
    others = list(range(n - 1, 0, -1))

    loads = [
        pltpu.make_async_copy(src, dst, load_sem.at[i])
        for i, (src, dst) in enumerate(
            [
                (key_hbm, key),
                (value_hbm, value),
                (ograd_hbm, ograd),
                (query_hbm, query),
                (filt_hbm, filt),
                (fwd_hbm, fwd),
                (inv_hbm, inv),
            ]
        )
    ]
    for load in loads[:4]:
        load.start()
    barrier = pltpu.get_barrier_semaphore()
    for d in others:
        pl.semaphore_signal(
            barrier, inc=1, device_id={"seq": partner(me, d, n)}, device_id_type=MESH
        )

    def columns(owner, half):
        return pl.ds(pl.multiple_of(owner * per_group + half * width, width), width)

    def row_block(owner):
        return pl.ds(pl.multiple_of(owner * rows, rows), rows)

    def gate(piece, owner):
        cols = columns(owner, piece // 2)
        one, two = (ograd, query) if piece % 2 else (key, value)
        return one[:, cols].astype(jnp.float32) * two[:, cols].astype(jnp.float32)

    half_len, half_rows = length // 2, rows // 2

    def parity_rows(parity, count):
        return pl.ds(parity, count, stride=2)

    def split_rows(piece, owner, slot):
        stage[slot] = gate(piece, owner).astype(jnp.bfloat16).astype(jnp.float32)
        return [
            stage[slot, parity_rows(parity, half_rows), :].astype(jnp.bfloat16)
            for parity in range(2)
        ]

    def half_block(owner):
        return pl.ds(pl.multiple_of(owner * half_rows, half_rows), half_rows)

    def fill(piece, d):
        for parity, values in enumerate(split_rows(piece, partner(me, d, n), d)):
            send[piece, d, parity] = values

    def out_copy(piece, d):
        return pltpu.make_async_remote_copy(
            src_ref=send.at[piece, d],
            dst_ref=arrived.at[piece, :, half_block(me)],
            send_sem=send_sem.at[0, piece, d],
            recv_sem=recv_sem.at[0, piece, d],
            device_id={"seq": partner(me, d, n)},
            device_id_type=MESH,
        )

    def back_copy(piece, d):
        return pltpu.make_async_remote_copy(
            src_ref=result.at[piece, row_block(partner(me, d, n))],
            dst_ref=back.at[piece, me],
            send_sem=send_sem.at[1, piece, d],
            recv_sem=recv_sem.at[1, piece, d],
            device_id={"seq": partner(me, d, n)},
            device_id_type=MESH,
        )

    pieces = range(2 * HALVES)
    sent = {}
    for piece in pieces:
        if piece < 2:
            loads[2 * piece].wait()
            loads[2 * piece + 1].wait()
        if piece == 0:
            for load in loads[4:]:
                load.start()
        for d in others:
            fill(piece, d)
            if piece == 0 and d == others[-1]:
                pl.semaphore_wait(barrier, n - 1)
                for e in others:
                    sent[0, 0, e] = out_copy(0, e)
                    sent[0, 0, e].start()
            elif piece > 0:
                sent[0, piece, d] = out_copy(piece, d)
                sent[0, piece, d].start()
    for piece in pieces:
        for parity, values in enumerate(split_rows(piece, me, 0)):
            arrived[piece, parity, half_block(me)] = values

    loads[4].wait()
    for i in range(HALVES):
        filt_t[i] = filt[i * width : (i + 1) * width, :].T
    loads[5].wait()
    every = slice(0, per_group)
    for parity in range(2):
        rows_now = parity_rows(parity, half_len)
        high, low = split_value(
            jnp.concatenate([filt_t[i, rows_now, :] for i in range(HALVES)], axis=1)
        )
        filt_raw[parity] = split_matmul(fwd[parity], high, low)
    chunk = min(64, half_len)
    chunks = [slice(start, start + chunk) for start in range(0, half_len, chunk)]
    for part in chunks:
        pairs = butterfly(filt_raw.at[0], filt_raw.at[1], part, every, half_len)
        for upper, pair in enumerate(pairs):
            for which in range(2):
                filt_spec[upper, which, part] = pair[which]
    loads[6].wait()

    def inverse_join(products):
        for parity in range(2):
            out = split_matmul(inv[parity], products[parity, 0], products[parity, 1])
            for i in range(out.shape[1] // width):
                joined[i, parity_rows(parity, half_len), :] = (
                    out[:, i * width : (i + 1) * width] * scale
                )

    every = slice(0, width)
    def filter_grad(half):
        for part in chunks:
            mixed, gated = [
                butterfly(spec.at[piece, 0], spec.at[piece, 1], part, every, half_len)
                for piece in (2 * half, 2 * half + 1)
            ]
            store_product(
                cross, part, every, half_len,
                times_conj(gated[0], mixed[0]), times_conj(gated[1], mixed[1]),
            )
        inverse_join(cross)
        held = pl.ds(half * width, width)
        fg[held, :] = joined[0].T
        return pltpu.make_async_copy(fg.at[held], fg_hbm.at[held], store_sem.at[len(pieces) + half])

    own = []
    for piece in pieces:
        for d in others:
            sent[0, piece, d].wait_recv()
        for parity in range(2):
            spec[piece, parity] = exact_matmul(fwd[parity], arrived[piece, parity])
        even, odd = spec.at[piece, 0], spec.at[piece, 1]
        fcols = slice((piece // 2) * width, (piece // 2 + 1) * width)
        multiply = times_conj if piece % 2 else times
        for part in chunks:
            data = butterfly(even, odd, part, every, half_len)
            lower, upper = [
                multiply(data[i], (filt_spec[i, 0, part, fcols], filt_spec[i, 1, part, fcols]))
                for i in range(2)
            ]
            store_product(prod, part, every, half_len, lower, upper)
        inverse_join(prod)
        result[piece] = joined[0].astype(jnp.bfloat16)
        for d in others:
            sent[1, piece, d] = back_copy(piece, d)
            sent[1, piece, d].start()
        own.append(
            pltpu.make_async_copy(
                result.at[piece, row_block(me)], back.at[piece, me], store_sem.at[piece]
            )
        )
        own[-1].start()
        if piece >= len(pieces) - HALVES:
            own.append(filter_grad(piece - (len(pieces) - HALVES)))
            own[-1].start()

    for piece in pieces:
        for d in others:
            sent[1, piece, d].wait_recv()
    for copy in sent.values():
        copy.wait_send()
    for store in own:
        store.wait()


def gate_kernel(
    key_hbm, value_hbm, ograd_hbm, back_hbm, fg_in, gq_hbm, gk_hbm, gv_hbm, fg_out,
    key, value, ograd, back, gq, gk, gv, fg, load_sem, store_sem,
):
    pieces, n, rows, width = back.shape
    halves = pieces // 2
    load_fg = pltpu.make_async_copy(fg_in, fg, load_sem.at[0, 4])
    store_fg = pltpu.make_async_copy(fg, fg_out, store_sem.at[0, 0])
    block = rows // GATE_STEPS
    loads = []
    for step in range(GATE_STEPS):
        part = pl.ds(step * block, block)
        pairs = [
            (back_hbm.at[:, :, part], back.at[:, :, part]),
            (key_hbm.at[part], key.at[part]),
            (value_hbm.at[part], value.at[part]),
            (ograd_hbm.at[part], ograd.at[part]),
        ]
        loads.append(
            [pltpu.make_async_copy(s, d, load_sem.at[step, i]) for i, (s, d) in enumerate(pairs)]
        )
        for load in loads[-1]:
            load.start()
        if step == 0:
            load_fg.start()
    stores = [store_fg]
    for step in range(GATE_STEPS):
        part = pl.ds(step * block, block)
        for load in loads[step]:
            load.wait()
        for owner in range(n):
            for half in range(halves):
                first = (owner * halves + half) * width
                cols = slice(first, first + width)
                conv = back[2 * half, owner, part].astype(jnp.float32)
                igrad = back[2 * half + 1, owner, part].astype(jnp.float32)
                gq[part, cols] = (ograd[part, cols].astype(jnp.float32) * conv).astype(gq.dtype)
                gk[part, cols] = (value[part, cols].astype(jnp.float32) * igrad).astype(gk.dtype)
                gv[part, cols] = (key[part, cols].astype(jnp.float32) * igrad).astype(gv.dtype)
        for i, (src, dst) in enumerate([(gq, gq_hbm), (gk, gk_hbm), (gv, gv_hbm)]):
            store = pltpu.make_async_copy(src.at[part], dst.at[part], store_sem.at[step, 1 + i])
            store.start()
            stores.append(store)
        if step == 0:
            load_fg.wait()
            store_fg.start()
    for store in stores:
        store.wait()


def fused(query, key_in, value, out_grad, filters):
    n = lax.axis_size("seq")
    rows, channels = query.shape
    per_group, length = filters.shape
    width = per_group // HALVES
    forward, inverse = dft_tables(length)
    bf16, f32 = jnp.bfloat16, jnp.float32
    gate = pltpu.VMEM((rows, channels), bf16)
    gate_shape = jax.ShapeDtypeStruct((rows, channels), bf16)
    back_shape = (2 * HALVES, n, rows, width)
    fg_shape = jax.ShapeDtypeStruct((per_group, length), f32)
    any_space = pl.BlockSpec(memory_space=pl.ANY)
    hbm = pl.BlockSpec(memory_space=pltpu.HBM)
    back, filter_grad = pl.pallas_call(
        functools.partial(fused_kernel, n),
        out_shape=(jax.ShapeDtypeStruct(back_shape, bf16), fg_shape),
        in_specs=[hbm] * 7,
        out_specs=(any_space,) * 2,
        scratch_shapes=[
            gate, gate, gate, gate,
            pltpu.VMEM((per_group, length), f32),
            pltpu.VMEM(forward.shape, bf16),
            pltpu.VMEM(inverse.shape, bf16),
            pltpu.VMEM((n, rows, width), f32),
            pltpu.VMEM((2 * HALVES, n, 2, rows // 2, width), bf16),
            pltpu.VMEM((2 * HALVES, 2, length // 2, width), bf16),
            pltpu.VMEM((HALVES, length, width), f32),
            pltpu.VMEM((2, length, per_group), f32),
            pltpu.VMEM((2, 2, length // 2, per_group), f32),
            pltpu.VMEM((2 * HALVES, 2, length, width), f32),
            pltpu.VMEM((2, 2, length, width), bf16),
            pltpu.VMEM((2, 2, length, width), bf16),
            pltpu.VMEM((HALVES, length, width), f32),
            pltpu.VMEM((2 * HALVES, length, width), bf16),
            pltpu.VMEM((per_group, length), f32),
            pltpu.SemaphoreType.DMA((7,)),
            pltpu.SemaphoreType.DMA((3 * HALVES,)),
            pltpu.SemaphoreType.DMA((2, 2 * HALVES, n)),
            pltpu.SemaphoreType.DMA((2, 2 * HALVES, n)),
        ],
        compiler_params=pltpu.CompilerParams(
            collective_id=0, has_side_effects=True, vmem_limit_bytes=VMEM_BYTES
        ),
        cost_estimate=pl.CostEstimate(
            flops=2 * 16 * 2 * length * length * per_group,
            bytes_accessed=12 * 1024 * 1024,
            transcendentals=0,
        ),
        name="hyena_bwd",
    )(key_in, value, out_grad, query, filters, jnp.asarray(forward), jnp.asarray(inverse))
    return pl.pallas_call(
        gate_kernel,
        out_shape=(gate_shape, gate_shape, gate_shape, fg_shape),
        in_specs=[hbm] * 3 + [any_space] * 2,
        out_specs=(hbm,) * 4,
        scratch_shapes=[
            gate, gate, gate,
            pltpu.VMEM(back_shape, bf16),
            gate, gate, gate,
            pltpu.VMEM((per_group, length), f32),
            pltpu.SemaphoreType.DMA((GATE_STEPS, 5)),
            pltpu.SemaphoreType.DMA((GATE_STEPS, 4)),
        ],
        compiler_params=pltpu.CompilerParams(vmem_limit_bytes=VMEM_BYTES),
        cost_estimate=pl.CostEstimate(
            flops=6 * rows * channels, bytes_accessed=4 * 1024 * 1024, transcendentals=0
        ),
        name="output_gates",
    )(key_in, value, out_grad, back, filter_grad)


def twiddle_tables(rows, cols, modulus, direction):
    row_index = lax.broadcasted_iota(jnp.int32, (rows, cols), 0)
    col_index = lax.broadcasted_iota(jnp.int32, (rows, cols), 1)
    angles = (
        direction * 2.0 * math.pi * (row_index * col_index % modulus).astype(jnp.float32) / modulus
    )
    return (jnp.cos(angles), jnp.sin(angles))


def complex_apply(real_part, imag_part, cosine, sines, form):
    highest = lax.Precision.HIGHEST
    out_real = jnp.einsum(form, real_part, cosine, precision=highest) - jnp.einsum(
        form, imag_part, sines, precision=highest
    )
    out_imag = jnp.einsum(form, real_part, sines, precision=highest) + jnp.einsum(
        form, imag_part, cosine, precision=highest
    )
    return (out_real, out_imag)


def transform(real_part, imag_part, direction):
    length = real_part.shape[-1]
    radix_one = math.gcd(length, 128)
    if length <= 256 or radix_one == 1:
        cosine, sines = twiddle_tables(length, length, length, direction)
        return complex_apply(real_part, imag_part, cosine, sines, "...j,kj->...k")
    radix_two = length // radix_one
    leading = real_part.shape[:-1]
    real_part = real_part.reshape(leading + (radix_one, radix_two))
    imag_part = imag_part.reshape(leading + (radix_one, radix_two))
    cosine, sines = twiddle_tables(radix_one, radix_one, radix_one, direction)
    real_part, imag_part = complex_apply(real_part, imag_part, cosine, sines, "...jm,kj->...km")
    cosine, sines = twiddle_tables(radix_one, radix_two, length, direction)
    real_part, imag_part = (
        real_part * cosine - imag_part * sines,
        real_part * sines + imag_part * cosine,
    )
    real_part, imag_part = transform(real_part, imag_part, direction)
    real_part = jnp.swapaxes(real_part, -1, -2).reshape(leading + (length,))
    imag_part = jnp.swapaxes(imag_part, -1, -2).reshape(leading + (length,))
    return (real_part, imag_part)


def mirrored(values):
    return jnp.roll(jnp.flip(values, -1), 1, -1)


def filter_work(mixed_part, gated_part, own_filter):
    length = mixed_part.shape[-1]
    padded_len = 2 * length
    factor = 1.0 / math.sqrt(length)

    def padded(values):
        widths = [(0, 0)] * (values.ndim - 1) + [(0, length)]
        return jnp.pad(values.astype(jnp.float32), widths)

    def inverse(real_part, imag_part):
        out_real, out_imag = transform(real_part, imag_part, 1.0)
        scale = factor / padded_len
        return (out_real[..., :length] * scale, out_imag[..., :length] * scale)

    both_re, both_im = transform(padded(mixed_part), padded(gated_part), -1.0)
    mirror_re, mirror_im = (mirrored(both_re), mirrored(both_im))
    mix_re = 0.5 * (both_re + mirror_re)
    mix_im = 0.5 * (both_im - mirror_im)
    gate_re = 0.5 * (both_im + mirror_im)
    gate_im = -0.5 * (both_re - mirror_re)
    filt_pad = padded(own_filter)
    filt_re, filt_im = transform(filt_pad, jnp.zeros_like(filt_pad), -1.0)
    conv_re = mix_re * filt_re - mix_im * filt_im
    conv_im = mix_re * filt_im + mix_im * filt_re
    back_re = gate_re * filt_re + gate_im * filt_im
    back_im = gate_im * filt_re - gate_re * filt_im
    conv_out, input_grad = inverse(conv_re - back_im, conv_im + back_re)
    filter_grad, unused = inverse(
        gate_re * mix_re + gate_im * mix_im, gate_im * mix_re - gate_re * mix_im
    )
    return (conv_out.astype(jnp.bfloat16), input_grad.astype(jnp.bfloat16), filter_grad)


def on_device(query, key_in, value, out_grad, filters):
    tok_rows, channels = query.shape
    groups = lax.axis_size("seq")
    per_group = channels // groups
    if groups & (groups - 1) == 0 and filters.shape[1] <= 1024 and per_group == 128 * HALVES and tok_rows % 32 == 0:
        return fused(query, key_in, value, out_grad, filters)
    mixed = (key_in.astype(jnp.float32) * value.astype(jnp.float32)).astype(jnp.bfloat16)
    gated = (out_grad.astype(jnp.float32) * query.astype(jnp.float32)).astype(jnp.bfloat16)
    send_mixed = mixed.T.reshape(groups, per_group, tok_rows)
    send_gated = gated.T.reshape(groups, per_group, tok_rows)
    own_filter = filters[None]
    arrived_mix, arrived_gate = (
        lax.all_to_all(send_mixed, "seq", split_axis=0, concat_axis=2, tiled=True),
        lax.all_to_all(send_gated, "seq", split_axis=0, concat_axis=2, tiled=True),
    )
    conv_out, input_grad, filter_grad = filter_work(arrived_mix, arrived_gate, own_filter)
    back_conv, back_grad = (
        lax.all_to_all(conv_out, "seq", split_axis=2, concat_axis=0, tiled=True),
        lax.all_to_all(input_grad, "seq", split_axis=2, concat_axis=0, tiled=True),
    )
    back_conv = back_conv.reshape(channels, tok_rows).T
    back_grad = back_grad.reshape(channels, tok_rows).T
    grad_query = (out_grad.astype(jnp.float32) * back_conv.astype(jnp.float32)).astype(jnp.bfloat16)
    grad_key = (back_grad.astype(jnp.float32) * value.astype(jnp.float32)).astype(jnp.bfloat16)
    grad_value = (back_grad.astype(jnp.float32) * key_in.astype(jnp.float32)).astype(jnp.bfloat16)
    return (grad_query, grad_key, grad_value, filter_grad[0])


def solution(mesh):
    placed = (
        P("seq", "ch"),
        P("seq", "ch"),
        P("seq", "ch"),
        P("seq", "ch"),
        P(("ch", "seq"), None),
    )
    return jax.shard_map(
        on_device,
        mesh=mesh,
        in_specs=placed,
        out_specs=(P("seq", "ch"), P("seq", "ch"), P("seq", "ch"), P(("ch", "seq"), None)),
        check_vma=False,
    )
```

```python
import functools
import math

import jax
import jax.numpy as jnp
import ml_dtypes
import numpy as np
from jax import lax
from jax.experimental import pallas as pl
from jax.experimental.pallas import tpu as pltpu
from jax.sharding import PartitionSpec as P

HALVES = 2
GATE_STEPS = 2
VMEM_BYTES = 63 * 1024 * 1024
MESH = pl.DeviceIdType.MESH


def split_bf16(table):
    high = table.astype(ml_dtypes.bfloat16)
    low = (table - high.astype(np.float64)).astype(ml_dtypes.bfloat16)
    return np.concatenate([high, low], axis=1)


def dft_tables(length):
    freq = 2 * np.arange(length // 2)[:, None] + 1
    forward, inverse = [], []
    for parity in range(2):
        time = np.arange(parity, length, 2)[None, :]
        angle = np.pi * ((freq * time) % (4 * length)) / (2 * length)
        table = np.concatenate([np.cos(angle), np.sin(angle)], axis=0)
        forward.append(split_bf16(table))
        inverse.append(split_bf16(np.ascontiguousarray(table.T)))
    return np.stack(forward), np.stack(inverse)


def split_value(values):
    high = values.astype(jnp.bfloat16)
    low = (values - high.astype(jnp.float32)).astype(jnp.bfloat16)
    return high, low


def matmul(a, b):
    return jnp.dot(a, b, preferred_element_type=jnp.float32)


def exact_matmul(table, data):
    return matmul(table, jnp.concatenate([data, data], axis=0))


def split_matmul(table, high, low):
    return exact_matmul(table, high) + matmul(table[:, : table.shape[1] // 2], low)


def butterfly(even, odd, rows, cols, half_len):
    sin_rows = slice(half_len + rows.start, half_len + rows.stop)
    even_cos, odd_cos = even[rows, cols], odd[rows, cols]
    even_sin, odd_sin = even[sin_rows, cols], odd[sin_rows, cols]
    return (
        (even_cos + odd_cos, even_sin + odd_sin),
        (even_cos - odd_cos, odd_sin - even_sin),
    )


def store_product(ref, rows, cols, half_len, lower, upper):
    sin_rows = slice(half_len + rows.start, half_len + rows.stop)
    values = (
        (0, rows, lower[0] + upper[0]),
        (0, sin_rows, lower[1] - upper[1]),
        (1, rows, lower[0] - upper[0]),
        (1, sin_rows, lower[1] + upper[1]),
    )
    for parity, to_rows, value in values:
        high, low = split_value(value)
        ref[parity, 0, to_rows, cols] = high
        ref[parity, 1, to_rows, cols] = low


def times(a, b):
    return a[0] * b[0] - a[1] * b[1], a[0] * b[1] + a[1] * b[0]


def times_conj(a, b):
    return a[0] * b[0] + a[1] * b[1], a[1] * b[0] - a[0] * b[1]


def partner(me, distance, n):
    total, bit = 0, 1
    while bit < n:
        digit = lax.rem(me // bit, 2)
        total = total + bit * (1 - digit if distance & bit else digit)
        bit *= 2
    return total


def fused_kernel(
    n,
    key_hbm, value_hbm, ograd_hbm, query_hbm, filt_hbm, fwd_hbm, inv_hbm,
    back, fg_hbm,
    key, value, ograd, query, filt, fwd, inv,
    stage, send, arrived, filt_t, filt_raw, filt_spec, spec, prod, cross, joined, result, fg,
    load_sem, store_sem, send_sem, recv_sem,
):
    rows, channels = key.shape
    per_group, length = filt.shape
    width = per_group // HALVES
    scale = 1.0 / (length * math.sqrt(length))
    me = lax.axis_index("seq")
    others = list(range(n - 1, 0, -1))

    loads = [
        pltpu.make_async_copy(src, dst, load_sem.at[i])
        for i, (src, dst) in enumerate(
            [
                (key_hbm, key),
                (value_hbm, value),
                (ograd_hbm, ograd),
                (query_hbm, query),
                (filt_hbm, filt),
                (fwd_hbm, fwd),
                (inv_hbm, inv),
            ]
        )
    ]
    for load in loads[:4]:
        load.start()
    barrier = pltpu.get_barrier_semaphore()
    for d in others:
        pl.semaphore_signal(
            barrier, inc=1, device_id={"seq": partner(me, d, n)}, device_id_type=MESH
        )

    def columns(owner, half):
        return pl.ds(pl.multiple_of(owner * per_group + half * width, width), width)

    def row_block(owner):
        return pl.ds(pl.multiple_of(owner * rows, rows), rows)

    def gate(piece, owner):
        cols = columns(owner, piece // 2)
        one, two = (ograd, query) if piece % 2 else (key, value)
        return one[:, cols].astype(jnp.float32) * two[:, cols].astype(jnp.float32)

    half_len, half_rows = length // 2, rows // 2

    def parity_rows(parity, count):
        return pl.ds(parity, count, stride=2)

    def split_rows(piece, owner, slot):
        stage[slot] = gate(piece, owner).astype(jnp.bfloat16).astype(jnp.float32)
        return [
            stage[slot, parity_rows(parity, half_rows), :].astype(jnp.bfloat16)
            for parity in range(2)
        ]

    def half_block(owner):
        return pl.ds(pl.multiple_of(owner * half_rows, half_rows), half_rows)

    def fill(piece, d):
        for parity, values in enumerate(split_rows(piece, partner(me, d, n), d)):
            send[piece, d, parity] = values

    def out_copy(piece, d):
        return pltpu.make_async_remote_copy(
            src_ref=send.at[piece, d],
            dst_ref=arrived.at[piece, :, half_block(me)],
            send_sem=send_sem.at[0, piece, d],
            recv_sem=recv_sem.at[0, piece, d],
            device_id={"seq": partner(me, d, n)},
            device_id_type=MESH,
        )

    def back_copy(piece, d):
        return pltpu.make_async_remote_copy(
            src_ref=result.at[piece, row_block(partner(me, d, n))],
            dst_ref=back.at[piece, me],
            send_sem=send_sem.at[1, piece, d],
            recv_sem=recv_sem.at[1, piece, d],
            device_id={"seq": partner(me, d, n)},
            device_id_type=MESH,
        )

    pieces = range(2 * HALVES)
    sent = {}
    for piece in pieces:
        if piece < 2:
            loads[2 * piece].wait()
            loads[2 * piece + 1].wait()
        if piece == 0:
            for load in loads[4:]:
                load.start()
        for d in others:
            fill(piece, d)
            if piece == 0 and d == others[-1]:
                pl.semaphore_wait(barrier, n - 1)
                for e in others:
                    sent[0, 0, e] = out_copy(0, e)
                    sent[0, 0, e].start()
            elif piece > 0:
                sent[0, piece, d] = out_copy(piece, d)
                sent[0, piece, d].start()
    for piece in pieces:
        for parity, values in enumerate(split_rows(piece, me, 0)):
            arrived[piece, parity, half_block(me)] = values

    loads[4].wait()
    for i in range(HALVES):
        filt_t[i] = filt[i * width : (i + 1) * width, :].T
    loads[5].wait()
    every = slice(0, per_group)
    for parity in range(2):
        rows_now = parity_rows(parity, half_len)
        high, low = split_value(
            jnp.concatenate([filt_t[i, rows_now, :] for i in range(HALVES)], axis=1)
        )
        filt_raw[parity] = split_matmul(fwd[parity], high, low)
    chunk = min(64, half_len)
    chunks = [slice(start, start + chunk) for start in range(0, half_len, chunk)]
    for part in chunks:
        pairs = butterfly(filt_raw.at[0], filt_raw.at[1], part, every, half_len)
        for upper, pair in enumerate(pairs):
            for which in range(2):
                filt_spec[upper, which, part] = pair[which]
    loads[6].wait()

    def inverse_join(products):
        for parity in range(2):
            out = split_matmul(inv[parity], products[parity, 0], products[parity, 1])
            for i in range(out.shape[1] // width):
                joined[i, parity_rows(parity, half_len), :] = (
                    out[:, i * width : (i + 1) * width] * scale
                )

    every = slice(0, width)
    def lanes(i):
        return slice(i * width, (i + 1) * width)

    groups = [tuple(pieces[:2])] + [(piece,) for piece in pieces[2:]]
    own = []
    for group in groups:
        for piece in group:
            for d in others:
                sent[0, piece, d].wait_recv()
        for parity in range(2):
            data = jnp.concatenate([arrived[piece, parity] for piece in group], axis=1)
            out = exact_matmul(fwd[parity], data)
            for i, piece in enumerate(group):
                spec[piece, parity] = out[:, lanes(i)]
        for i, piece in enumerate(group):
            fcols = lanes(piece // 2)
            multiply = times_conj if piece % 2 else times
            for part in chunks:
                data = butterfly(spec.at[piece, 0], spec.at[piece, 1], part, every, half_len)
                lower, upper = [
                    multiply(data[j], (filt_spec[j, 0, part, fcols], filt_spec[j, 1, part, fcols]))
                    for j in range(2)
                ]
                store_product(prod, part, lanes(i), half_len, lower, upper)
        inverse_join(prod.at[:, :, :, : len(group) * width])
        for i, piece in enumerate(group):
            result[piece] = joined[i].astype(jnp.bfloat16)
            for d in others:
                sent[1, piece, d] = back_copy(piece, d)
                sent[1, piece, d].start()
            own.append(
                pltpu.make_async_copy(
                    result.at[piece, row_block(me)], back.at[piece, me], store_sem.at[piece]
                )
            )
            own[-1].start()

    for half in range(HALVES):
        for part in chunks:
            mixed, gated = [
                butterfly(spec.at[piece, 0], spec.at[piece, 1], part, every, half_len)
                for piece in (2 * half, 2 * half + 1)
            ]
            store_product(
                cross, part, lanes(half), half_len,
                times_conj(gated[0], mixed[0]), times_conj(gated[1], mixed[1]),
            )
    inverse_join(cross)
    for i in range(HALVES):
        fg[lanes(i), :] = joined[i].T
    own.append(pltpu.make_async_copy(fg, fg_hbm, store_sem.at[len(pieces)]))
    own[-1].start()

    for piece in pieces:
        for d in others:
            sent[1, piece, d].wait_recv()
    for copy in sent.values():
        copy.wait_send()
    for store in own:
        store.wait()


def gate_kernel(
    key_hbm, value_hbm, ograd_hbm, back_hbm, fg_in, gq_hbm, gk_hbm, gv_hbm, fg_out,
    key, value, ograd, back, gq, gk, gv, fg, load_sem, store_sem,
):
    pieces, n, rows, width = back.shape
    halves = pieces // 2
    load_fg = pltpu.make_async_copy(fg_in, fg, load_sem.at[0, 4])
    store_fg = pltpu.make_async_copy(fg, fg_out, store_sem.at[0, 0])
    block = rows // GATE_STEPS
    loads = []
    for step in range(GATE_STEPS):
        part = pl.ds(step * block, block)
        pairs = [
            (back_hbm.at[:, :, part], back.at[:, :, part]),
            (key_hbm.at[part], key.at[part]),
            (value_hbm.at[part], value.at[part]),
            (ograd_hbm.at[part], ograd.at[part]),
        ]
        loads.append(
            [pltpu.make_async_copy(s, d, load_sem.at[step, i]) for i, (s, d) in enumerate(pairs)]
        )
        for load in loads[-1]:
            load.start()
        if step == 0:
            load_fg.start()
    stores = [store_fg]
    for step in range(GATE_STEPS):
        part = pl.ds(step * block, block)
        for load in loads[step]:
            load.wait()
        for owner in range(n):
            for half in range(halves):
                first = (owner * halves + half) * width
                cols = slice(first, first + width)
                conv = back[2 * half, owner, part].astype(jnp.float32)
                igrad = back[2 * half + 1, owner, part].astype(jnp.float32)
                gq[part, cols] = (ograd[part, cols].astype(jnp.float32) * conv).astype(gq.dtype)
                gk[part, cols] = (value[part, cols].astype(jnp.float32) * igrad).astype(gk.dtype)
                gv[part, cols] = (key[part, cols].astype(jnp.float32) * igrad).astype(gv.dtype)
        for i, (src, dst) in enumerate([(gq, gq_hbm), (gk, gk_hbm), (gv, gv_hbm)]):
            store = pltpu.make_async_copy(src.at[part], dst.at[part], store_sem.at[step, 1 + i])
            store.start()
            stores.append(store)
        if step == 0:
            load_fg.wait()
            store_fg.start()
    for store in stores:
        store.wait()


def fused(query, key_in, value, out_grad, filters):
    n = lax.axis_size("seq")
    rows, channels = query.shape
    per_group, length = filters.shape
    width = per_group // HALVES
    forward, inverse = dft_tables(length)
    bf16, f32 = jnp.bfloat16, jnp.float32
    gate = pltpu.VMEM((rows, channels), bf16)
    gate_shape = jax.ShapeDtypeStruct((rows, channels), bf16)
    back_shape = (2 * HALVES, n, rows, width)
    fg_shape = jax.ShapeDtypeStruct((per_group, length), f32)
    any_space = pl.BlockSpec(memory_space=pl.ANY)
    hbm = pl.BlockSpec(memory_space=pltpu.HBM)
    back, filter_grad = pl.pallas_call(
        functools.partial(fused_kernel, n),
        out_shape=(jax.ShapeDtypeStruct(back_shape, bf16), fg_shape),
        in_specs=[hbm] * 7,
        out_specs=(any_space,) * 2,
        scratch_shapes=[
            gate, gate, gate, gate,
            pltpu.VMEM((per_group, length), f32),
            pltpu.VMEM(forward.shape, bf16),
            pltpu.VMEM(inverse.shape, bf16),
            pltpu.VMEM((n, rows, width), f32),
            pltpu.VMEM((2 * HALVES, n, 2, rows // 2, width), bf16),
            pltpu.VMEM((2 * HALVES, 2, length // 2, width), bf16),
            pltpu.VMEM((HALVES, length, width), f32),
            pltpu.VMEM((2, length, per_group), f32),
            pltpu.VMEM((2, 2, length // 2, per_group), f32),
            pltpu.VMEM((2 * HALVES, 2, length, width), f32),
            pltpu.VMEM((2, 2, length, per_group), bf16),
            pltpu.VMEM((2, 2, length, per_group), bf16),
            pltpu.VMEM((HALVES, length, width), f32),
            pltpu.VMEM((2 * HALVES, length, width), bf16),
            pltpu.VMEM((per_group, length), f32),
            pltpu.SemaphoreType.DMA((7,)),
            pltpu.SemaphoreType.DMA((1 + 2 * HALVES,)),
            pltpu.SemaphoreType.DMA((2, 2 * HALVES, n)),
            pltpu.SemaphoreType.DMA((2, 2 * HALVES, n)),
        ],
        compiler_params=pltpu.CompilerParams(
            collective_id=0, has_side_effects=True, vmem_limit_bytes=VMEM_BYTES
        ),
        cost_estimate=pl.CostEstimate(
            flops=2 * 16 * 2 * length * length * per_group,
            bytes_accessed=12 * 1024 * 1024,
            transcendentals=0,
        ),
        name="hyena_bwd",
    )(key_in, value, out_grad, query, filters, jnp.asarray(forward), jnp.asarray(inverse))
    return pl.pallas_call(
        gate_kernel,
        out_shape=(gate_shape, gate_shape, gate_shape, fg_shape),
        in_specs=[hbm] * 3 + [any_space] * 2,
        out_specs=(hbm,) * 4,
        scratch_shapes=[
            gate, gate, gate,
            pltpu.VMEM(back_shape, bf16),
            gate, gate, gate,
            pltpu.VMEM((per_group, length), f32),
            pltpu.SemaphoreType.DMA((GATE_STEPS, 5)),
            pltpu.SemaphoreType.DMA((GATE_STEPS, 4)),
        ],
        compiler_params=pltpu.CompilerParams(vmem_limit_bytes=VMEM_BYTES),
        cost_estimate=pl.CostEstimate(
            flops=6 * rows * channels, bytes_accessed=4 * 1024 * 1024, transcendentals=0
        ),
        name="output_gates",
    )(key_in, value, out_grad, back, filter_grad)


def twiddle_tables(rows, cols, modulus, direction):
    row_index = lax.broadcasted_iota(jnp.int32, (rows, cols), 0)
    col_index = lax.broadcasted_iota(jnp.int32, (rows, cols), 1)
    angles = (
        direction * 2.0 * math.pi * (row_index * col_index % modulus).astype(jnp.float32) / modulus
    )
    return (jnp.cos(angles), jnp.sin(angles))


def complex_apply(real_part, imag_part, cosine, sines, form):
    highest = lax.Precision.HIGHEST
    out_real = jnp.einsum(form, real_part, cosine, precision=highest) - jnp.einsum(
        form, imag_part, sines, precision=highest
    )
    out_imag = jnp.einsum(form, real_part, sines, precision=highest) + jnp.einsum(
        form, imag_part, cosine, precision=highest
    )
    return (out_real, out_imag)


def transform(real_part, imag_part, direction):
    length = real_part.shape[-1]
    radix_one = math.gcd(length, 128)
    if length <= 256 or radix_one == 1:
        cosine, sines = twiddle_tables(length, length, length, direction)
        return complex_apply(real_part, imag_part, cosine, sines, "...j,kj->...k")
    radix_two = length // radix_one
    leading = real_part.shape[:-1]
    real_part = real_part.reshape(leading + (radix_one, radix_two))
    imag_part = imag_part.reshape(leading + (radix_one, radix_two))
    cosine, sines = twiddle_tables(radix_one, radix_one, radix_one, direction)
    real_part, imag_part = complex_apply(real_part, imag_part, cosine, sines, "...jm,kj->...km")
    cosine, sines = twiddle_tables(radix_one, radix_two, length, direction)
    real_part, imag_part = (
        real_part * cosine - imag_part * sines,
        real_part * sines + imag_part * cosine,
    )
    real_part, imag_part = transform(real_part, imag_part, direction)
    real_part = jnp.swapaxes(real_part, -1, -2).reshape(leading + (length,))
    imag_part = jnp.swapaxes(imag_part, -1, -2).reshape(leading + (length,))
    return (real_part, imag_part)


def mirrored(values):
    return jnp.roll(jnp.flip(values, -1), 1, -1)


def filter_work(mixed_part, gated_part, own_filter):
    length = mixed_part.shape[-1]
    padded_len = 2 * length
    factor = 1.0 / math.sqrt(length)

    def padded(values):
        widths = [(0, 0)] * (values.ndim - 1) + [(0, length)]
        return jnp.pad(values.astype(jnp.float32), widths)

    def inverse(real_part, imag_part):
        out_real, out_imag = transform(real_part, imag_part, 1.0)
        scale = factor / padded_len
        return (out_real[..., :length] * scale, out_imag[..., :length] * scale)

    both_re, both_im = transform(padded(mixed_part), padded(gated_part), -1.0)
    mirror_re, mirror_im = (mirrored(both_re), mirrored(both_im))
    mix_re = 0.5 * (both_re + mirror_re)
    mix_im = 0.5 * (both_im - mirror_im)
    gate_re = 0.5 * (both_im + mirror_im)
    gate_im = -0.5 * (both_re - mirror_re)
    filt_pad = padded(own_filter)
    filt_re, filt_im = transform(filt_pad, jnp.zeros_like(filt_pad), -1.0)
    conv_re = mix_re * filt_re - mix_im * filt_im
    conv_im = mix_re * filt_im + mix_im * filt_re
    back_re = gate_re * filt_re + gate_im * filt_im
    back_im = gate_im * filt_re - gate_re * filt_im
    conv_out, input_grad = inverse(conv_re - back_im, conv_im + back_re)
    filter_grad, unused = inverse(
        gate_re * mix_re + gate_im * mix_im, gate_im * mix_re - gate_re * mix_im
    )
    return (conv_out.astype(jnp.bfloat16), input_grad.astype(jnp.bfloat16), filter_grad)


def on_device(query, key_in, value, out_grad, filters):
    tok_rows, channels = query.shape
    groups = lax.axis_size("seq")
    per_group = channels // groups
    if groups & (groups - 1) == 0 and filters.shape[1] <= 1024 and per_group == 128 * HALVES and tok_rows % 32 == 0:
        return fused(query, key_in, value, out_grad, filters)
    mixed = (key_in.astype(jnp.float32) * value.astype(jnp.float32)).astype(jnp.bfloat16)
    gated = (out_grad.astype(jnp.float32) * query.astype(jnp.float32)).astype(jnp.bfloat16)
    send_mixed = mixed.T.reshape(groups, per_group, tok_rows)
    send_gated = gated.T.reshape(groups, per_group, tok_rows)
    own_filter = filters[None]
    arrived_mix, arrived_gate = (
        lax.all_to_all(send_mixed, "seq", split_axis=0, concat_axis=2, tiled=True),
        lax.all_to_all(send_gated, "seq", split_axis=0, concat_axis=2, tiled=True),
    )
    conv_out, input_grad, filter_grad = filter_work(arrived_mix, arrived_gate, own_filter)
    back_conv, back_grad = (
        lax.all_to_all(conv_out, "seq", split_axis=2, concat_axis=0, tiled=True),
        lax.all_to_all(input_grad, "seq", split_axis=2, concat_axis=0, tiled=True),
    )
    back_conv = back_conv.reshape(channels, tok_rows).T
    back_grad = back_grad.reshape(channels, tok_rows).T
    grad_query = (out_grad.astype(jnp.float32) * back_conv.astype(jnp.float32)).astype(jnp.bfloat16)
    grad_key = (back_grad.astype(jnp.float32) * value.astype(jnp.float32)).astype(jnp.bfloat16)
    grad_value = (back_grad.astype(jnp.float32) * key_in.astype(jnp.float32)).astype(jnp.bfloat16)
    return (grad_query, grad_key, grad_value, filter_grad[0])


def solution(mesh):
    placed = (
        P("seq", "ch"),
        P("seq", "ch"),
        P("seq", "ch"),
        P("seq", "ch"),
        P(("ch", "seq"), None),
    )
    return jax.shard_map(
        on_device,
        mesh=mesh,
        in_specs=placed,
        out_specs=(P("seq", "ch"), P("seq", "ch"), P("seq", "ch"), P(("ch", "seq"), None)),
        check_vma=False,
    )
```

```python
import functools
import math

import jax
import jax.numpy as jnp
import ml_dtypes
import numpy as np
from jax import lax
from jax.experimental import pallas as pl
from jax.experimental.pallas import tpu as pltpu
from jax.sharding import PartitionSpec as P

HALVES = 2
GATE_STEPS = 4
VMEM_BYTES = 63 * 1024 * 1024
MESH = pl.DeviceIdType.MESH


def split_bf16(table):
    high = table.astype(ml_dtypes.bfloat16)
    low = (table - high.astype(np.float64)).astype(ml_dtypes.bfloat16)
    return np.concatenate([high, low], axis=1)


def dft_tables(length):
    freq = 2 * np.arange(length // 2)[:, None] + 1
    forward, inverse = [], []
    for parity in range(2):
        time = np.arange(parity, length, 2)[None, :]
        angle = np.pi * ((freq * time) % (4 * length)) / (2 * length)
        table = np.concatenate([np.cos(angle), np.sin(angle)], axis=0)
        forward.append(split_bf16(table))
        inverse.append(split_bf16(np.ascontiguousarray(table.T)))
    return np.stack(forward), np.stack(inverse)


def split_value(values):
    high = values.astype(jnp.bfloat16)
    low = (values - high.astype(jnp.float32)).astype(jnp.bfloat16)
    return high, low


def matmul(a, b):
    return jnp.dot(a, b, preferred_element_type=jnp.float32)


def exact_matmul(table, data):
    return matmul(table, jnp.concatenate([data, data], axis=0))


def split_matmul(table, high, low):
    tables = jnp.concatenate([table, table[:, : table.shape[1] // 2]], axis=1)
    return matmul(tables, jnp.concatenate([high, high, low], axis=0))


def butterfly(even, odd, rows, cols, half_len):
    sin_rows = slice(half_len + rows.start, half_len + rows.stop)
    even_cos, odd_cos = even[rows, cols], odd[rows, cols]
    even_sin, odd_sin = even[sin_rows, cols], odd[sin_rows, cols]
    return (
        (even_cos + odd_cos, even_sin + odd_sin),
        (even_cos - odd_cos, odd_sin - even_sin),
    )


def store_product(ref, rows, cols, half_len, lower, upper):
    sin_rows = slice(half_len + rows.start, half_len + rows.stop)
    values = (
        (0, rows, lower[0] + upper[0]),
        (0, sin_rows, lower[1] - upper[1]),
        (1, rows, lower[0] - upper[0]),
        (1, sin_rows, lower[1] + upper[1]),
    )
    for parity, to_rows, value in values:
        high, low = split_value(value)
        ref[parity, 0, to_rows, cols] = high
        ref[parity, 1, to_rows, cols] = low


def times(a, b):
    return a[0] * b[0] - a[1] * b[1], a[0] * b[1] + a[1] * b[0]


def times_conj(a, b):
    return a[0] * b[0] + a[1] * b[1], a[1] * b[0] - a[0] * b[1]


def partner(me, distance, n):
    total, bit = 0, 1
    while bit < n:
        digit = lax.rem(me // bit, 2)
        total = total + bit * (1 - digit if distance & bit else digit)
        bit *= 2
    return total


def fused_kernel(
    n,
    key_hbm, value_hbm, ograd_hbm, query_hbm, filt_hbm, fwd_hbm, inv_hbm,
    back, fg_hbm,
    key, value, ograd, query, filt, fwd, inv,
    stage, send, arrived, filt_t, filt_raw, filt_spec, spec, prod, cross, joined, result, fg,
    load_sem, store_sem, send_sem, recv_sem,
):
    rows, channels = key.shape
    per_group, length = filt.shape
    width = per_group // HALVES
    scale = 1.0 / (length * math.sqrt(length))
    me = lax.axis_index("seq")
    others = list(range(n - 1, 0, -1))

    loads = [
        pltpu.make_async_copy(src, dst, load_sem.at[i])
        for i, (src, dst) in enumerate(
            [
                (key_hbm, key),
                (value_hbm, value),
                (ograd_hbm, ograd),
                (query_hbm, query),
                (filt_hbm, filt),
                (fwd_hbm, fwd),
                (inv_hbm, inv),
            ]
        )
    ]
    for load in loads[:4]:
        load.start()
    barrier = pltpu.get_barrier_semaphore()
    for d in others:
        pl.semaphore_signal(
            barrier, inc=1, device_id={"seq": partner(me, d, n)}, device_id_type=MESH
        )

    def columns(owner, half):
        return pl.ds(pl.multiple_of(owner * per_group + half * width, width), width)

    def row_block(owner):
        return pl.ds(pl.multiple_of(owner * rows, rows), rows)

    def gate(piece, owner):
        cols = columns(owner, piece // 2)
        one, two = (ograd, query) if piece % 2 else (key, value)
        return one[:, cols].astype(jnp.float32) * two[:, cols].astype(jnp.float32)

    half_len, half_rows = length // 2, rows // 2

    def parity_rows(parity, count):
        return pl.ds(parity, count, stride=2)

    def split_rows(piece, owner, slot):
        stage[slot] = gate(piece, owner).astype(jnp.bfloat16).astype(jnp.float32)
        return [
            stage[slot, parity_rows(parity, half_rows), :].astype(jnp.bfloat16)
            for parity in range(2)
        ]

    def half_block(owner):
        return pl.ds(pl.multiple_of(owner * half_rows, half_rows), half_rows)

    def fill(piece, d):
        for parity, values in enumerate(split_rows(piece, partner(me, d, n), d)):
            send[piece, d, parity] = values

    def out_copy(piece, d):
        return pltpu.make_async_remote_copy(
            src_ref=send.at[piece, d],
            dst_ref=arrived.at[piece, :, half_block(me)],
            send_sem=send_sem.at[0, piece, d],
            recv_sem=recv_sem.at[0, piece, d],
            device_id={"seq": partner(me, d, n)},
            device_id_type=MESH,
        )

    def back_copy(piece, d):
        return pltpu.make_async_remote_copy(
            src_ref=result.at[piece, row_block(partner(me, d, n))],
            dst_ref=back.at[piece, me],
            send_sem=send_sem.at[1, piece, d],
            recv_sem=recv_sem.at[1, piece, d],
            device_id={"seq": partner(me, d, n)},
            device_id_type=MESH,
        )

    pieces = range(2 * HALVES)
    sent = {}
    for piece in pieces:
        if piece < 2:
            loads[2 * piece].wait()
            loads[2 * piece + 1].wait()
        if piece == 0:
            for load in loads[4:]:
                load.start()
        for d in others:
            fill(piece, d)
            if piece == 0 and d == others[-1]:
                pl.semaphore_wait(barrier, n - 1)
                for e in others:
                    sent[0, 0, e] = out_copy(0, e)
                    sent[0, 0, e].start()
            elif piece > 0:
                sent[0, piece, d] = out_copy(piece, d)
                sent[0, piece, d].start()
    for piece in pieces:
        for parity, values in enumerate(split_rows(piece, me, 0)):
            arrived[piece, parity, half_block(me)] = values

    loads[4].wait()
    for i in range(HALVES):
        filt_t[i] = filt[i * width : (i + 1) * width, :].T
    loads[5].wait()
    every = slice(0, per_group)
    for parity in range(2):
        rows_now = parity_rows(parity, half_len)
        high, low = split_value(
            jnp.concatenate([filt_t[i, rows_now, :] for i in range(HALVES)], axis=1)
        )
        filt_raw[parity] = split_matmul(fwd[parity], high, low)
    chunk = min(64, half_len)
    chunks = [slice(start, start + chunk) for start in range(0, half_len, chunk)]
    for part in chunks:
        pairs = butterfly(filt_raw.at[0], filt_raw.at[1], part, every, half_len)
        for upper, pair in enumerate(pairs):
            for which in range(2):
                filt_spec[upper, which, part] = pair[which]
    loads[6].wait()

    def inverse_join(products):
        for parity in range(2):
            out = split_matmul(inv[parity], products[parity, 0], products[parity, 1])
            for i in range(out.shape[1] // width):
                joined[i, parity_rows(parity, half_len), :] = (
                    out[:, i * width : (i + 1) * width] * scale
                )

    every = slice(0, width)
    def lanes(i):
        return slice(i * width, (i + 1) * width)

    groups = [tuple(pieces[:2])] + [(piece,) for piece in pieces[2:]]
    own = []
    for group in groups:
        for piece in group:
            for d in others:
                sent[0, piece, d].wait_recv()
        for parity in range(2):
            data = jnp.concatenate([arrived[piece, parity] for piece in group], axis=1)
            out = exact_matmul(fwd[parity], data)
            for i, piece in enumerate(group):
                spec[piece, parity] = out[:, lanes(i)]
        for i, piece in enumerate(group):
            fcols = lanes(piece // 2)
            multiply = times_conj if piece % 2 else times
            for part in chunks:
                data = butterfly(spec.at[piece, 0], spec.at[piece, 1], part, every, half_len)
                lower, upper = [
                    multiply(data[j], (filt_spec[j, 0, part, fcols], filt_spec[j, 1, part, fcols]))
                    for j in range(2)
                ]
                store_product(prod, part, lanes(i), half_len, lower, upper)
        inverse_join(prod.at[:, :, :, : len(group) * width])
        for i, piece in enumerate(group):
            result[piece] = joined[i].astype(jnp.bfloat16)
            for d in others:
                sent[1, piece, d] = back_copy(piece, d)
                sent[1, piece, d].start()
            own.append(
                pltpu.make_async_copy(
                    result.at[piece, row_block(me)], back.at[piece, me], store_sem.at[piece]
                )
            )
            own[-1].start()

    for half in range(HALVES):
        for part in chunks:
            mixed, gated = [
                butterfly(spec.at[piece, 0], spec.at[piece, 1], part, every, half_len)
                for piece in (2 * half, 2 * half + 1)
            ]
            store_product(
                cross, part, lanes(half), half_len,
                times_conj(gated[0], mixed[0]), times_conj(gated[1], mixed[1]),
            )
    inverse_join(cross)
    for i in range(HALVES):
        fg[lanes(i), :] = joined[i].T
    own.append(pltpu.make_async_copy(fg, fg_hbm, store_sem.at[len(pieces)]))
    own[-1].start()

    for piece in pieces:
        for d in others:
            sent[1, piece, d].wait_recv()
    for copy in sent.values():
        copy.wait_send()
    for store in own:
        store.wait()


def gate_kernel(
    key_hbm, value_hbm, ograd_hbm, back_hbm, fg_in, gq_hbm, gk_hbm, gv_hbm, fg_out,
    key, value, ograd, back, gq, gk, gv, fg, load_sem, store_sem,
):
    pieces, n, rows, width = back.shape
    halves = pieces // 2
    load_fg = pltpu.make_async_copy(fg_in, fg, load_sem.at[0, 4])
    store_fg = pltpu.make_async_copy(fg, fg_out, store_sem.at[0, 0])
    block = rows // GATE_STEPS
    loads = []
    for step in range(GATE_STEPS):
        part = pl.ds(step * block, block)
        pairs = [
            (back_hbm.at[:, :, part], back.at[:, :, part]),
            (key_hbm.at[part], key.at[part]),
            (value_hbm.at[part], value.at[part]),
            (ograd_hbm.at[part], ograd.at[part]),
        ]
        loads.append(
            [pltpu.make_async_copy(s, d, load_sem.at[step, i]) for i, (s, d) in enumerate(pairs)]
        )
        for load in loads[-1]:
            load.start()
        if step == 0:
            load_fg.start()
    stores = [store_fg]
    for step in range(GATE_STEPS):
        part = pl.ds(step * block, block)
        for load in loads[step]:
            load.wait()
        for owner in range(n):
            for half in range(halves):
                first = (owner * halves + half) * width
                cols = slice(first, first + width)
                conv = back[2 * half, owner, part].astype(jnp.float32)
                igrad = back[2 * half + 1, owner, part].astype(jnp.float32)
                gq[part, cols] = (ograd[part, cols].astype(jnp.float32) * conv).astype(gq.dtype)
                gk[part, cols] = (value[part, cols].astype(jnp.float32) * igrad).astype(gk.dtype)
                gv[part, cols] = (key[part, cols].astype(jnp.float32) * igrad).astype(gv.dtype)
        for i, (src, dst) in enumerate([(gq, gq_hbm), (gk, gk_hbm), (gv, gv_hbm)]):
            store = pltpu.make_async_copy(src.at[part], dst.at[part], store_sem.at[step, 1 + i])
            store.start()
            stores.append(store)
        if step == 0:
            load_fg.wait()
            store_fg.start()
    for store in stores:
        store.wait()


def fused(query, key_in, value, out_grad, filters):
    n = lax.axis_size("seq")
    rows, channels = query.shape
    per_group, length = filters.shape
    width = per_group // HALVES
    forward, inverse = dft_tables(length)
    bf16, f32 = jnp.bfloat16, jnp.float32
    gate = pltpu.VMEM((rows, channels), bf16)
    gate_shape = jax.ShapeDtypeStruct((rows, channels), bf16)
    back_shape = (2 * HALVES, n, rows, width)
    fg_shape = jax.ShapeDtypeStruct((per_group, length), f32)
    any_space = pl.BlockSpec(memory_space=pl.ANY)
    hbm = pl.BlockSpec(memory_space=pltpu.HBM)
    back, filter_grad = pl.pallas_call(
        functools.partial(fused_kernel, n),
        out_shape=(jax.ShapeDtypeStruct(back_shape, bf16), fg_shape),
        in_specs=[hbm] * 7,
        out_specs=(any_space,) * 2,
        scratch_shapes=[
            gate, gate, gate, gate,
            pltpu.VMEM((per_group, length), f32),
            pltpu.VMEM(forward.shape, bf16),
            pltpu.VMEM(inverse.shape, bf16),
            pltpu.VMEM((n, rows, width), f32),
            pltpu.VMEM((2 * HALVES, n, 2, rows // 2, width), bf16),
            pltpu.VMEM((2 * HALVES, 2, length // 2, width), bf16),
            pltpu.VMEM((HALVES, length, width), f32),
            pltpu.VMEM((2, length, per_group), f32),
            pltpu.VMEM((2, 2, length // 2, per_group), f32),
            pltpu.VMEM((2 * HALVES, 2, length, width), f32),
            pltpu.VMEM((2, 2, length, per_group), bf16),
            pltpu.VMEM((2, 2, length, per_group), bf16),
            pltpu.VMEM((HALVES, length, width), f32),
            pltpu.VMEM((2 * HALVES, length, width), bf16),
            pltpu.VMEM((per_group, length), f32),
            pltpu.SemaphoreType.DMA((7,)),
            pltpu.SemaphoreType.DMA((1 + 2 * HALVES,)),
            pltpu.SemaphoreType.DMA((2, 2 * HALVES, n)),
            pltpu.SemaphoreType.DMA((2, 2 * HALVES, n)),
        ],
        compiler_params=pltpu.CompilerParams(
            collective_id=0, has_side_effects=True, vmem_limit_bytes=VMEM_BYTES
        ),
        cost_estimate=pl.CostEstimate(
            flops=2 * 16 * 2 * length * length * per_group,
            bytes_accessed=12 * 1024 * 1024,
            transcendentals=0,
        ),
        name="hyena_bwd",
    )(key_in, value, out_grad, query, filters, jnp.asarray(forward), jnp.asarray(inverse))
    return pl.pallas_call(
        gate_kernel,
        out_shape=(gate_shape, gate_shape, gate_shape, fg_shape),
        in_specs=[hbm] * 3 + [any_space] * 2,
        out_specs=(hbm,) * 4,
        scratch_shapes=[
            gate, gate, gate,
            pltpu.VMEM(back_shape, bf16),
            gate, gate, gate,
            pltpu.VMEM((per_group, length), f32),
            pltpu.SemaphoreType.DMA((GATE_STEPS, 5)),
            pltpu.SemaphoreType.DMA((GATE_STEPS, 4)),
        ],
        compiler_params=pltpu.CompilerParams(vmem_limit_bytes=VMEM_BYTES),
        cost_estimate=pl.CostEstimate(
            flops=6 * rows * channels, bytes_accessed=4 * 1024 * 1024, transcendentals=0
        ),
        name="output_gates",
    )(key_in, value, out_grad, back, filter_grad)


def twiddle_tables(rows, cols, modulus, direction):
    row_index = lax.broadcasted_iota(jnp.int32, (rows, cols), 0)
    col_index = lax.broadcasted_iota(jnp.int32, (rows, cols), 1)
    angles = (
        direction * 2.0 * math.pi * (row_index * col_index % modulus).astype(jnp.float32) / modulus
    )
    return (jnp.cos(angles), jnp.sin(angles))


def complex_apply(real_part, imag_part, cosine, sines, form):
    highest = lax.Precision.HIGHEST
    out_real = jnp.einsum(form, real_part, cosine, precision=highest) - jnp.einsum(
        form, imag_part, sines, precision=highest
    )
    out_imag = jnp.einsum(form, real_part, sines, precision=highest) + jnp.einsum(
        form, imag_part, cosine, precision=highest
    )
    return (out_real, out_imag)


def transform(real_part, imag_part, direction):
    length = real_part.shape[-1]
    radix_one = math.gcd(length, 128)
    if length <= 256 or radix_one == 1:
        cosine, sines = twiddle_tables(length, length, length, direction)
        return complex_apply(real_part, imag_part, cosine, sines, "...j,kj->...k")
    radix_two = length // radix_one
    leading = real_part.shape[:-1]
    real_part = real_part.reshape(leading + (radix_one, radix_two))
    imag_part = imag_part.reshape(leading + (radix_one, radix_two))
    cosine, sines = twiddle_tables(radix_one, radix_one, radix_one, direction)
    real_part, imag_part = complex_apply(real_part, imag_part, cosine, sines, "...jm,kj->...km")
    cosine, sines = twiddle_tables(radix_one, radix_two, length, direction)
    real_part, imag_part = (
        real_part * cosine - imag_part * sines,
        real_part * sines + imag_part * cosine,
    )
    real_part, imag_part = transform(real_part, imag_part, direction)
    real_part = jnp.swapaxes(real_part, -1, -2).reshape(leading + (length,))
    imag_part = jnp.swapaxes(imag_part, -1, -2).reshape(leading + (length,))
    return (real_part, imag_part)


def mirrored(values):
    return jnp.roll(jnp.flip(values, -1), 1, -1)


def filter_work(mixed_part, gated_part, own_filter):
    length = mixed_part.shape[-1]
    padded_len = 2 * length
    factor = 1.0 / math.sqrt(length)

    def padded(values):
        widths = [(0, 0)] * (values.ndim - 1) + [(0, length)]
        return jnp.pad(values.astype(jnp.float32), widths)

    def inverse(real_part, imag_part):
        out_real, out_imag = transform(real_part, imag_part, 1.0)
        scale = factor / padded_len
        return (out_real[..., :length] * scale, out_imag[..., :length] * scale)

    both_re, both_im = transform(padded(mixed_part), padded(gated_part), -1.0)
    mirror_re, mirror_im = (mirrored(both_re), mirrored(both_im))
    mix_re = 0.5 * (both_re + mirror_re)
    mix_im = 0.5 * (both_im - mirror_im)
    gate_re = 0.5 * (both_im + mirror_im)
    gate_im = -0.5 * (both_re - mirror_re)
    filt_pad = padded(own_filter)
    filt_re, filt_im = transform(filt_pad, jnp.zeros_like(filt_pad), -1.0)
    conv_re = mix_re * filt_re - mix_im * filt_im
    conv_im = mix_re * filt_im + mix_im * filt_re
    back_re = gate_re * filt_re + gate_im * filt_im
    back_im = gate_im * filt_re - gate_re * filt_im
    conv_out, input_grad = inverse(conv_re - back_im, conv_im + back_re)
    filter_grad, unused = inverse(
        gate_re * mix_re + gate_im * mix_im, gate_im * mix_re - gate_re * mix_im
    )
    return (conv_out.astype(jnp.bfloat16), input_grad.astype(jnp.bfloat16), filter_grad)


def on_device(query, key_in, value, out_grad, filters):
    tok_rows, channels = query.shape
    groups = lax.axis_size("seq")
    per_group = channels // groups
    if groups & (groups - 1) == 0 and filters.shape[1] <= 1024 and per_group == 128 * HALVES and tok_rows % 32 == 0:
        return fused(query, key_in, value, out_grad, filters)
    mixed = (key_in.astype(jnp.float32) * value.astype(jnp.float32)).astype(jnp.bfloat16)
    gated = (out_grad.astype(jnp.float32) * query.astype(jnp.float32)).astype(jnp.bfloat16)
    send_mixed = mixed.T.reshape(groups, per_group, tok_rows)
    send_gated = gated.T.reshape(groups, per_group, tok_rows)
    own_filter = filters[None]
    arrived_mix, arrived_gate = (
        lax.all_to_all(send_mixed, "seq", split_axis=0, concat_axis=2, tiled=True),
        lax.all_to_all(send_gated, "seq", split_axis=0, concat_axis=2, tiled=True),
    )
    conv_out, input_grad, filter_grad = filter_work(arrived_mix, arrived_gate, own_filter)
    back_conv, back_grad = (
        lax.all_to_all(conv_out, "seq", split_axis=2, concat_axis=0, tiled=True),
        lax.all_to_all(input_grad, "seq", split_axis=2, concat_axis=0, tiled=True),
    )
    back_conv = back_conv.reshape(channels, tok_rows).T
    back_grad = back_grad.reshape(channels, tok_rows).T
    grad_query = (out_grad.astype(jnp.float32) * back_conv.astype(jnp.float32)).astype(jnp.bfloat16)
    grad_key = (back_grad.astype(jnp.float32) * value.astype(jnp.float32)).astype(jnp.bfloat16)
    grad_value = (back_grad.astype(jnp.float32) * key_in.astype(jnp.float32)).astype(jnp.bfloat16)
    return (grad_query, grad_key, grad_value, filter_grad[0])


def solution(mesh):
    placed = (
        P("seq", "ch"),
        P("seq", "ch"),
        P("seq", "ch"),
        P("seq", "ch"),
        P(("ch", "seq"), None),
    )
    return jax.shard_map(
        on_device,
        mesh=mesh,
        in_specs=placed,
        out_specs=(P("seq", "ch"), P("seq", "ch"), P("seq", "ch"), P(("ch", "seq"), None)),
        check_vma=False,
    )
```
